512 devices in a mesh: row: 32 (over x_hi, z, core), col: 16 (over y, x_lo).
Axes of the slice: x: 4 (x_hi: 2, x_lo: 2; x = x_hi * 2 + x_lo), y: 8, z: 8, core: 2. Of those that a mesh axis runs over, the one named last changes fastest.
Arguments:
- ancestor_inverse: float32 [12288, 12288], P('row', 'col'), may hold values from -6 to 6
- panel: float32 [4096, 512], P('col', 'row'), may hold values from -0.09375 to 0.09375
- unit_inverse: float32 [512, 512], P('row'), may hold values from -1 to 1, as said below
- pivot_inverse: float32 [512, 512], P('row', 'col'), may hold values from -6 to 6
- panel_blocks: int32 [32], replicated, may hold values from 0 to 95, as said below
Outputs:
- inverse_row: float32 [512, 12288], P('col', 'row')
- diagonal_block: float32 [512, 512], P('row', 'col')
The draws below stay inside these ranges and needn't reach their ends.
Inputs may be any that keep to these rules, and one draw needn't show every extreme that they name: `panel_blocks`: Distinct, in no particular order. Among the window blocks c * 6 to c * 6 + 5 of any process column c at most 3 are listed, and exactly 3 for some columns. `unit_inverse`: unit lower triangular: ones on the diagonal, zeros above it.
All inputs are finite; a program needn't handle non-finite values.
Results may differ from the reference program's by a relative error of at most 0.00011.
Values sent between devices are 32-bit elements; how exact they have to be, the bound alone decides.
No kernel may reach another device: no remote copies, remote signals or barrier semaphores. Data moves between devices by JAX's collectives and lax.ppermute only.
A program may use at most 64 MiB of HBM per device.

```python
import jax
import jax.numpy as jnp
from jax import lax

W = 512
BLK = 128
NWB = 96
R = 12288
PB = 32
P_SIZE = 4096
N_COL = 16


def draw_panel_blocks(key, part):
    range_blocks = NWB // N_COL
    slot_count = range_blocks // 2
    column_order = jax.random.permutation(jax.random.fold_in(key, 11), N_COL)
    counts_used = jnp.where(column_order % 2 == 0, slot_count, slot_count - 2)
    base_ranks = jnp.tile(jnp.arange(range_blocks, dtype=jnp.int32)[None, :], (N_COL, 1))
    ranks = jax.random.permutation(jax.random.fold_in(key, 12), base_ranks, axis=1, independent=True)
    chosen = ranks < counts_used[:, None]
    first_local = jnp.argmax(chosen.astype(jnp.int32), axis=1).astype(jnp.int32)
    firsts = jnp.arange(N_COL, dtype=jnp.int32) * range_blocks + first_local
    local_ids = jnp.arange(range_blocks, dtype=jnp.int32)[None, :]
    rest_mask = (chosen & (local_ids != first_local[:, None])).reshape(-1).astype(jnp.int32)
    per_shard = PB // N_COL
    rest_ids = jnp.argsort(1 - rest_mask, stable=True)[:PB - N_COL].astype(jnp.int32)
    rest_part = rest_ids.reshape(N_COL, per_shard - 1)
    leading = jnp.roll(firsts, -(N_COL // 2))
    stored = jnp.concatenate([leading[:, None], rest_part], axis=1).reshape(-1)
    return stored.astype(jnp.int32)


def draw_unit_inverse(key, part):
    spread = 0.5 / W ** 0.5
    entries = jax.random.truncated_normal(jax.random.fold_in(key, 21), -4.0, 4.0, (W, W), jnp.float32) * spread
    row_ids = jnp.arange(W, dtype=jnp.int32)[:, None]
    col_ids = jnp.arange(W, dtype=jnp.int32)[None, :]
    below = jnp.where(row_ids > col_ids, entries, 0.0)
    return (below + jnp.where(row_ids == col_ids, 1.0, 0.0)).astype(jnp.float32)


def block_scale(stream_key, extent, shards, low, high):
    factor_of, own = 1.0, jax.random.fold_in(stream_key, 6)
    for axis_at, shards_of in shards:
        steps = jnp.exp(jax.random.uniform(jax.random.fold_in(own, axis_at), (shards_of,), jnp.float32, low / len(shards), high / len(shards)))
        factor_of = factor_of * jnp.repeat(steps, extent[axis_at] // shards_of).reshape([-1 if axis == axis_at else 1 for axis in range(len(extent))])
    return factor_of


def bell_draw(rng, dims, width, bound, split=(), kind=jnp.bfloat16):
    drawn = width * jax.random.normal(rng, dims, jnp.float32)
    if split:
        drawn = drawn * block_scale(rng, dims, split, -0.22, 0.18)
    return jnp.clip(drawn, -bound, bound).astype(kind)


def setup_inputs(seed: int = 0) -> dict:
    streams_of = jax.random.split(jax.random.key(seed), 6)
    return {
        "ancestor_inverse": bell_draw(streams_of[0], (R, R), 1.0, 6.0, ((0, 32), (1, 16)), jnp.float32),
        "panel": bell_draw(streams_of[1], (P_SIZE, W), P_SIZE ** -0.5, 0.09375, ((0, 16), (1, 32)), jnp.float32),
        "unit_inverse": draw_unit_inverse(jax.random.fold_in(streams_of[5], 71), 0),
        "pivot_inverse": bell_draw(streams_of[3], (W, W), 1.0, 6.0, ((0, 32), (1, 16)), jnp.float32),
        "panel_blocks": draw_panel_blocks(jax.random.fold_in(streams_of[5], 71), 0),
    }


def reference(ancestor_inverse, panel, unit_inverse, pivot_inverse, panel_blocks):
    highest = lax.Precision.HIGHEST
    normal = jnp.dot(panel, unit_inverse, precision=highest, preferred_element_type=jnp.float32)
    blocked = ancestor_inverse.reshape(R, NWB, BLK)
    columns = jnp.take(blocked, panel_blocks, axis=1).reshape(R, PB * BLK)
    column_inverse = -jnp.dot(columns, normal, precision=highest, preferred_element_type=jnp.float32)
    listed = jnp.take(column_inverse.reshape(NWB, BLK, W), panel_blocks, axis=0).reshape(PB * BLK, W)
    product = jnp.dot(normal.T, listed, precision=highest, preferred_element_type=jnp.float32)
    diagonal_block = pivot_inverse - product
    return column_inverse.T, diagonal_block
```

```python
import jax
import jax.numpy as jnp
from jax import lax
from jax.experimental import pallas as pl
from jax.experimental.pallas import tpu as pltpu
from jax.sharding import Mesh
from jax.sharding import PartitionSpec as P

BLK = 128
SLOTS = 3
ROW = ("x_hi", "z", "core")
CHIPS = ("x_hi", "z")
COL = ("y", "x_lo")
PARAMS = pltpu.CompilerParams(vmem_limit_bytes=32 * 1024 * 1024)
VMEM = pl.BlockSpec(memory_space=pltpu.VMEM)
SMEM = pl.BlockSpec(memory_space=pltpu.SMEM)


def split(value):
    high = value.astype(jnp.bfloat16)
    low = (value - high.astype(jnp.float32)).astype(jnp.bfloat16)
    return high, low


def product(left, right, dims):
    left_high, left_low = split(left)
    right_high, right_low = split(right)

    def dot(a, b):
        return lax.dot_general(a, b, (dims, ((), ())), preferred_element_type=jnp.float32)

    return dot(left_high, right_high) + (dot(left_high, right_low) + dot(left_low, right_high))


def pack_kernel(slots, place, stored, unit, out):
    here = place[0]
    chips, rows, _ = out.shape
    span = SLOTS * BLK

    def block(slot):
        index = slots[slot]
        safe = jnp.maximum(index, 0)
        lane = pl.multiple_of(lax.rem(safe, 2) * BLK, BLK)
        value = stored[lax.div(safe, 2), :, pl.ds(lane, BLK)]
        return jnp.where(index >= 0, value, 0.0)

    mine = jnp.concatenate([block(here * SLOTS + s) for s in range(SLOTS)], axis=1)
    unit_rows = unit[...]
    for chip in range(chips):
        out[chip, :, 0:span] = mine
        out[chip, :, 2 * span :] = unit_rows
        for s in range(SLOTS):
            out[chip, :, span + s * BLK : span + (s + 1) * BLK] = block(chip * SLOTS + s)


def normal_kernel(gathered, col_out, row_out):
    span = SLOTS * BLK
    unit = gathered[:, 2 * span :].T
    col_out[...] = product(unit, gathered[:, :span], ((1,), (0,)))
    row_out[...] = product(unit, gathered[:, span : 2 * span], ((1,), (0,)))


def window_kernel(blocks, own, other, inverse, out):
    total = None
    for s in range(SLOTS):
        lane = pl.multiple_of(jnp.maximum(blocks[s], 0) * BLK, BLK)
        at = slice(s * BLK, (s + 1) * BLK)
        value = product(own[:, at] + other[:, at], inverse[:, pl.ds(lane, BLK)], ((1,), (1,)))
        total = value if total is None else total + value
    out[...] = total


def diagonal_kernel(blocks, own, other, arrived, tile_out, out):
    tile = arrived[0]
    for c in range(1, arrived.shape[0]):
        tile = tile + arrived[c]
    tile_out[...] = -tile
    total = None
    for s in range(SLOTS):
        place = blocks[s]
        lane = pl.multiple_of(jnp.maximum(place, 0) * BLK, BLK)
        at = slice(s * BLK, (s + 1) * BLK)
        listed = jnp.where(place >= 0, tile_out[:, pl.ds(lane, BLK)], 0.0)
        value = product(own[:, at] + other[:, at], listed, ((1,), (1,)))
        total = value if total is None else total + value
    rows = out.shape[0]
    width = total.shape[1]
    total = total.reshape(rows, 2, 8, width)
    pad = jnp.zeros((rows, 8, 128 - 2 * width), jnp.float32)
    out[...] = jnp.concatenate([total[:, 0], total[:, 1], pad], axis=2)


def final_kernel(arrived, pivot, out):
    total = arrived[0]
    for r in range(1, arrived.shape[0]):
        total = total + arrived[r]
    width = out.shape[1]
    out[0:8, :] = pivot[0:8, :] - total[:, 0:width]
    out[8:16, :] = pivot[8:16, :] - total[:, width : 2 * width]


def call(kernel, shapes, specs, flops=0, moved=0):
    return pl.pallas_call(
        kernel,
        out_shape=shapes,
        in_specs=specs,
        out_specs=jax.tree.map(lambda _: VMEM, shapes),
        compiler_params=PARAMS,
        cost_estimate=pl.CostEstimate(flops=flops, bytes_accessed=moved, transcendentals=0),
    )


def f32(*shape):
    return jax.ShapeDtypeStruct(shape, jnp.float32)


def on_device(ancestor_inverse, panel, unit_inverse, pivot_inverse, panel_blocks):
    chip = lax.axis_index(CHIPS)
    core = lax.axis_index("core")
    col = lax.axis_index(COL)
    cols = lax.axis_size(COL)
    chips = lax.axis_size(CHIPS)
    rows_here, cols_here = ancestor_inverse.shape
    unit_rows, width = unit_inverse.shape
    range_blocks = cols_here // BLK
    row_blocks = rows_here // BLK
    span = SLOTS * BLK
    total_blocks = panel_blocks.shape[0]

    owner = panel_blocks // range_blocks
    order = jnp.arange(total_blocks, dtype=jnp.int32)
    same = (owner[:, None] == owner[None, :]) & (order[None, :] < order[:, None])
    slot_of = owner * SLOTS + jnp.sum(same.astype(jnp.int32), axis=1)
    all_slots = jnp.arange(cols * SLOTS, dtype=jnp.int32)
    hit = (slot_of[None, :] == all_slots[:, None]).astype(jnp.int32)
    slots = jnp.sum(hit * (order + 1)[None, :], axis=1) - 1
    window = jnp.sum(hit * (panel_blocks + 1)[None, :], axis=1) - 1
    col_blocks = lax.dynamic_slice(window, (col * SLOTS,), (SLOTS,)) - col * range_blocks
    own_blocks = lax.dynamic_slice(window, (chip * SLOTS,), (SLOTS,))
    own_blocks = own_blocks - chip * range_blocks - core * row_blocks
    own_blocks = jnp.where(own_blocks < row_blocks, own_blocks, -1)
    place = col.reshape(1).astype(jnp.int32)

    stored = jnp.broadcast_to(panel.T[None], (cols, panel.shape[1], panel.shape[0]))
    stored = lax.all_to_all(stored, COL, 0, 0, tiled=True)
    payload = call(
        pack_kernel,
        f32(chips, unit_rows, 2 * span + width),
        [SMEM, SMEM, VMEM, VMEM],
        moved=2 * 1024 * 1024,
    )(slots, place, stored, unit_inverse)
    gathered = lax.all_to_all(payload, CHIPS, 0, 0, tiled=True)
    gathered = gathered.reshape(chips * unit_rows, 2 * span + width)
    col_own, row_own = call(
        normal_kernel,
        (f32(width, span), f32(width, span)),
        [VMEM],
        flops=2 * 3 * chips * unit_rows * width * 2 * span,
        moved=3 * 1024 * 1024,
    )(gathered)
    swap = [(0, 1), (1, 0)]
    col_other = lax.ppermute(col_own, "core", swap)
    row_other = lax.ppermute(row_own, "core", swap)
    partial_tile = call(
        window_kernel,
        f32(width, rows_here),
        [SMEM, VMEM, VMEM, VMEM],
        flops=2 * 3 * width * span * rows_here,
        moved=3 * 1024 * 1024,
    )(col_blocks, col_own, col_other, ancestor_inverse)
    partial_tile = partial_tile.reshape(cols, width // cols, rows_here)
    arrived = lax.all_to_all(partial_tile, COL, 0, 0, tiled=True)
    row_count = lax.axis_size(ROW)
    inverse_tile, share = call(
        diagonal_kernel,
        (f32(width // cols, rows_here), f32(row_count, 8, 128)),
        [SMEM, VMEM, VMEM, VMEM],
        flops=2 * 3 * width * span * (width // cols),
        moved=3 * 1024 * 1024,
    )(own_blocks, row_own, row_other, arrived)
    shares = lax.all_to_all(share, ROW, 0, 0, tiled=True)
    diagonal_block = call(
        final_kernel, f32(*pivot_inverse.shape), [VMEM, VMEM], moved=1024 * 128
    )(shares, pivot_inverse)
    return (inverse_tile, diagonal_block)


def solution(mesh):
    finer = Mesh(
        mesh.devices.reshape(2, mesh.shape["row"] // 4, 2, mesh.shape["col"] // 2, 2),
        (*ROW, *COL),
    )
    return jax.shard_map(
        on_device,
        mesh=finer,
        in_specs=(P(ROW, COL), P(COL, ROW), P(ROW, None), P(ROW, COL), P()),
        out_specs=(P(COL, ROW), P(ROW, COL)),
        check_vma=False,
    )
```

```python
import jax
import jax.numpy as jnp
from jax import lax
from jax.experimental import pallas as pl
from jax.experimental.pallas import tpu as pltpu
from jax.sharding import Mesh
from jax.sharding import PartitionSpec as P

BLK = 128
SLOTS = 3
ROW = ("x_hi", "z", "core")
CHIPS = ("x_hi", "z")
COL = ("y", "x_lo")
PARAMS = pltpu.CompilerParams(vmem_limit_bytes=32 * 1024 * 1024)
VMEM = pl.BlockSpec(memory_space=pltpu.VMEM)
SMEM = pl.BlockSpec(memory_space=pltpu.SMEM)


def split(value):
    high = value.astype(jnp.bfloat16)
    low = (value - high.astype(jnp.float32)).astype(jnp.bfloat16)
    return high, low


def left_parts(value):
    high, low = split(value)
    return jnp.concatenate([high, high, low], axis=1)


def right_parts(value):
    high, low = split(value)
    return jnp.concatenate([high, low, high], axis=0)


def dot(left, right):
    return jnp.dot(left, right, preferred_element_type=jnp.float32)


def pack_kernel(slots, place, stored, out):
    here, half = place[0], place[1]
    chips = out.shape[0]
    rows = stored.shape[1]

    def block(slot, start, count):
        index = slots[slot]
        safe = jnp.maximum(index, 0)
        lane = pl.multiple_of(lax.rem(safe, 2) * BLK, BLK)
        value = stored[lax.div(safe, 2), pl.ds(start, count), pl.ds(lane, BLK)]
        return jnp.where(index >= 0, value, 0.0)

    mine = jnp.concatenate([block(here * SLOTS + s, 0, rows) for s in range(SLOTS)], axis=1)
    start = pl.multiple_of(half * (rows // 2), rows // 2)
    for chip in range(chips):
        out[chip, 0:rows, :] = mine
        for s in range(SLOTS):
            out[chip, rows:, s * BLK : (s + 1) * BLK] = block(chip * SLOTS + s, start, rows // 2)


def inverse_kernel(blocks, inverse, out):
    listed = []
    for s in range(SLOTS):
        lane = pl.multiple_of(jnp.maximum(blocks[s], 0) * BLK, BLK)
        listed.append(inverse[:, pl.ds(lane, BLK)].T)
    out[...] = right_parts(jnp.concatenate(listed, axis=0))


def unit_kernel(place, near, far, out):
    chip = place[2]
    count = near.shape[0]
    pieces = []
    for source in range(2 * count):
        bits = lax.bitwise_xor(chip, source)
        at = (
            lax.bitwise_and(lax.shift_right_logical(bits, 2), 1)
            + lax.bitwise_and(bits, 2)
            + lax.bitwise_and(bits, 1) * 4
        )
        value = jnp.where(bits < count, near[at], far[at])
        pieces.append(value.T)
    out[...] = left_parts(jnp.concatenate(pieces, axis=1))


def normal_kernel(unit, gathered, out):
    chips, _, span = gathered.shape
    rows = unit.shape[1] // (3 * chips)
    out[...] = dot(unit[...], right_parts(gathered[:, :rows, :].reshape(chips * rows, span)))


def row_normal_kernel(place, unit, own, other, out):
    chips, half, span = own.shape
    first = place[1] == 0
    low = jnp.where(first, own[...], other[...])
    high = jnp.where(first, other[...], own[...])
    listed = jnp.concatenate([low, high], axis=1).reshape(chips * 2 * half, span)
    out[...] = dot(unit[...], right_parts(listed))


def window_kernel(inverse, own, other, out):
    out[...] = dot(left_parts(own[...] + other[...]), inverse[...])


def diagonal_kernel(blocks, own, other, arrived, tile_out, out):
    tile = arrived[0]
    for c in range(1, arrived.shape[0]):
        tile = tile + arrived[c]
    tile_out[...] = -tile
    listed = []
    for s in range(SLOTS):
        place = blocks[s]
        lane = pl.multiple_of(jnp.maximum(place, 0) * BLK, BLK)
        listed.append(jnp.where(place >= 0, tile_out[:, pl.ds(lane, BLK)], 0.0).T)
    total = dot(left_parts(own[...] + other[...]), right_parts(jnp.concatenate(listed, axis=0)))
    rows = out.shape[0]
    width = total.shape[1]
    total = total.reshape(rows, 2, 8, width)
    pad = jnp.zeros((rows, 8, 128 - 2 * width), jnp.float32)
    out[...] = jnp.concatenate([total[:, 0], total[:, 1], pad], axis=2)


def final_kernel(arrived, pivot, out):
    total = arrived[0]
    for r in range(1, arrived.shape[0]):
        total = total + arrived[r]
    width = out.shape[1]
    out[0:8, :] = pivot[0:8, :] - total[:, 0:width]
    out[8:16, :] = pivot[8:16, :] - total[:, width : 2 * width]


def call(kernel, shapes, specs, flops=0, moved=0):
    return pl.pallas_call(
        kernel,
        out_shape=shapes,
        in_specs=specs,
        out_specs=jax.tree.map(lambda _: VMEM, shapes),
        compiler_params=PARAMS,
        cost_estimate=pl.CostEstimate(flops=flops, bytes_accessed=moved, transcendentals=0),
    )


def f32(*shape):
    return jax.ShapeDtypeStruct(shape, jnp.float32)


def on_device(ancestor_inverse, panel, unit_inverse, pivot_inverse, panel_blocks):
    chip = lax.axis_index(CHIPS)
    core = lax.axis_index("core")
    col = lax.axis_index(COL)
    cols = lax.axis_size(COL)
    chips = lax.axis_size(CHIPS)
    rows_here, cols_here = ancestor_inverse.shape
    unit_rows, width = unit_inverse.shape
    range_blocks = cols_here // BLK
    row_blocks = rows_here // BLK
    span = SLOTS * BLK
    total_blocks = panel_blocks.shape[0]

    owner = panel_blocks // range_blocks
    order = jnp.arange(total_blocks, dtype=jnp.int32)
    same = (owner[:, None] == owner[None, :]) & (order[None, :] < order[:, None])
    slot_of = owner * SLOTS + jnp.sum(same.astype(jnp.int32), axis=1)
    all_slots = jnp.arange(cols * SLOTS, dtype=jnp.int32)
    hit = (slot_of[None, :] == all_slots[:, None]).astype(jnp.int32)
    slots = jnp.sum(hit * (order + 1)[None, :], axis=1) - 1
    window = jnp.sum(hit * (panel_blocks + 1)[None, :], axis=1) - 1
    col_blocks = lax.dynamic_slice(window, (col * SLOTS,), (SLOTS,)) - col * range_blocks
    own_blocks = lax.dynamic_slice(window, (chip * SLOTS,), (SLOTS,))
    own_blocks = own_blocks - chip * range_blocks - core * row_blocks
    own_blocks = jnp.where(own_blocks < row_blocks, own_blocks, -1)
    x_lo = lax.axis_index("x_lo")
    place = jnp.stack([col, x_lo, chip]).astype(jnp.int32)
    swap = [(0, 1), (1, 0)]

    stored = jnp.broadcast_to(panel.T[None], (cols, panel.shape[1], panel.shape[0]))
    stored = lax.all_to_all(stored, COL, 0, 0, tiled=True)

    near = unit_inverse[None]
    for step in (4, 2, 1):
        pairs = [(z, z ^ step) for z in range(lax.axis_size("z"))]
        near = jnp.concatenate([near, lax.ppermute(near, "z", pairs)], axis=0)
        if step == 2:
            near, stored = lax.optimization_barrier((near, stored))
    far = lax.ppermute(near, "x_hi", swap)

    payload = call(
        pack_kernel,
        f32(chips, unit_rows + unit_rows // 2, span),
        [SMEM, SMEM, VMEM],
        moved=1024 * 1024,
    )(slots, place, stored)
    gathered = lax.all_to_all(payload, CHIPS, 0, 0, tiled=True)
    inverse = call(
        inverse_kernel,
        jax.ShapeDtypeStruct((3 * span, rows_here), jnp.bfloat16),
        [SMEM, VMEM],
        moved=3 * 1024 * 1024,
    )(col_blocks, ancestor_inverse)
    unit = call(
        unit_kernel,
        jax.ShapeDtypeStruct((width, 3 * chips * unit_rows), jnp.bfloat16),
        [SMEM, VMEM, VMEM],
        moved=2 * 1024 * 1024,
    )(place, near, far)
    flops = 2 * 3 * chips * unit_rows * width * span
    col_own = call(normal_kernel, f32(width, span), [VMEM, VMEM], flops, 2 * 1024 * 1024)(unit, gathered)
    col_other = lax.ppermute(col_own, "core", swap)
    partial_tile = call(
        window_kernel,
        f32(width, rows_here),
        [VMEM, VMEM, VMEM],
        flops=2 * 3 * width * span * rows_here,
        moved=3 * 1024 * 1024,
    )(inverse, col_own, col_other)
    partial_tile, half_own = lax.optimization_barrier((partial_tile, gathered[:, unit_rows:, :]))
    half_other = lax.ppermute(half_own, "x_lo", swap)
    row_own = call(
        row_normal_kernel, f32(width, span), [SMEM, VMEM, VMEM, VMEM], flops, 2 * 1024 * 1024
    )(place, unit, half_own, half_other)
    row_other = lax.ppermute(row_own, "core", swap)
    partial_tile = partial_tile.reshape(cols, width // cols, rows_here)
    arrived = lax.all_to_all(partial_tile, COL, 0, 0, tiled=True)
    row_count = lax.axis_size(ROW)
    inverse_tile, share = call(
        diagonal_kernel,
        (f32(width // cols, rows_here), f32(row_count, 8, 128)),
        [SMEM, VMEM, VMEM, VMEM],
        flops=2 * 3 * width * span * (width // cols),
        moved=3 * 1024 * 1024,
    )(own_blocks, row_own, row_other, arrived)
    shares = lax.all_to_all(share, ROW, 0, 0, tiled=True)
    diagonal_block = call(
        final_kernel, f32(*pivot_inverse.shape), [VMEM, VMEM], moved=1024 * 128
    )(shares, pivot_inverse)
    return (inverse_tile, diagonal_block)


def solution(mesh):
    finer = Mesh(
        mesh.devices.reshape(2, mesh.shape["row"] // 4, 2, mesh.shape["col"] // 2, 2),
        (*ROW, *COL),
    )
    return jax.shard_map(
        on_device,
        mesh=finer,
        in_specs=(P(ROW, COL), P(COL, ROW), P(ROW, None), P(ROW, COL), P()),
        out_specs=(P(COL, ROW), P(ROW, COL)),
        check_vma=False,
    )
```

```python
import jax
import jax.numpy as jnp
from jax import lax
from jax.experimental import pallas as pl
from jax.experimental.pallas import tpu as pltpu
from jax.sharding import Mesh
from jax.sharding import PartitionSpec as P

BLK = 128
SLOTS = 3
ROW = ("x_hi", "z", "core")
CHIPS = ("x_hi", "z")
COL = ("y", "x_lo")
PARAMS = pltpu.CompilerParams(vmem_limit_bytes=12 * 1024 * 1024)
VMEM = pl.BlockSpec(memory_space=pltpu.VMEM)
SMEM = pl.BlockSpec(memory_space=pltpu.SMEM)


def split(value):
    high = value.astype(jnp.bfloat16)
    low = (value - high.astype(jnp.float32)).astype(jnp.bfloat16)
    return high, low


def left_parts(value):
    high, low = split(value)
    return jnp.concatenate([high, high, low], axis=1)


def right_parts(value):
    high, low = split(value)
    return jnp.concatenate([high, low, high], axis=0)


def dot(left, right):
    return jnp.dot(left, right, preferred_element_type=jnp.float32)


def spread_kernel(panel, out):
    value = panel[...]
    for col in range(out.shape[0]):
        out[col] = value


def unit_kernel(unit, out):
    rows, width = unit.shape
    half = rows // 2
    start = out.shape[2] - 2 * width
    value = unit[...]
    for chip in range(out.shape[0]):
        out[chip, :, start : start + width] = value[:half]
        out[chip, :, start + width :] = value[half:]


def pack_kernel(slots, place, stored, before, out):
    del before
    here, half = place[0], place[1]
    chips = out.shape[0]
    rows = stored.shape[1] // 2
    span = SLOTS * BLK

    def block(slot, start):
        index = slots[slot]
        safe = jnp.maximum(index, 0)
        lane = pl.multiple_of(lax.rem(safe, 2) * BLK, BLK)
        value = stored[lax.div(safe, 2), pl.ds(start, rows), pl.ds(lane, BLK)]
        return jnp.where(index >= 0, value, 0.0)

    mine = [block(here * SLOTS + s, part * rows) for part in range(2) for s in range(SLOTS)]
    mine = jnp.concatenate(mine, axis=1)
    start = pl.multiple_of(half * rows, rows)
    for chip in range(chips):
        out[chip, :, : 2 * span] = mine
        for s in range(SLOTS):
            at = 2 * span + s * BLK
            out[chip, :, at : at + BLK] = block(chip * SLOTS + s, start)


def unit_parts(gathered, width):
    start = gathered.shape[1] - 2 * width
    unit = jnp.concatenate([gathered[:, start : start + width], gathered[:, start + width :]], axis=0)
    return left_parts(unit.T)


def inverse_kernel(blocks, inverse, out):
    listed = []
    for s in range(SLOTS):
        lane = pl.multiple_of(jnp.maximum(blocks[s], 0) * BLK, BLK)
        listed.append(inverse[:, pl.ds(lane, BLK)].T)
    out[...] = right_parts(jnp.concatenate(listed, axis=0))


def normal_kernel(gathered, out):
    width, span = out.shape
    listed = jnp.concatenate([gathered[:, :span], gathered[:, span : 2 * span]], axis=0)
    out[...] = dot(unit_parts(gathered, width), right_parts(listed))


def row_normal_kernel(place, gathered, own, other, out):
    first = place[1] == 0
    low = jnp.where(first, own[...], other[...])
    high = jnp.where(first, other[...], own[...])
    listed = jnp.concatenate([low, high], axis=0)
    out[...] = dot(unit_parts(gathered, out.shape[0]), right_parts(listed))


def row_sum_kernel(own, other, out):
    out[...] = left_parts(own[...] + other[...])


def window_kernel(inverse, own, other, out):
    out[...] = dot(left_parts(own[...] + other[...]), inverse[...])


def diagonal_kernel(blocks, normal, arrived, tile_out, out):
    tile = arrived[0]
    for c in range(1, arrived.shape[0]):
        tile = tile + arrived[c]
    tile_out[...] = -tile
    listed = []
    for s in range(SLOTS):
        place = blocks[s]
        lane = pl.multiple_of(jnp.maximum(place, 0) * BLK, BLK)
        listed.append(jnp.where(place >= 0, tile_out[:, pl.ds(lane, BLK)], 0.0).T)
    total = dot(normal[...], right_parts(jnp.concatenate(listed, axis=0)))
    rows = out.shape[0]
    width = total.shape[1]
    total = total.reshape(rows, 2, 8, width)
    pad = jnp.zeros((rows, 8, 128 - 2 * width), jnp.float32)
    out[...] = jnp.concatenate([total[:, 0], total[:, 1], pad], axis=2)


def final_kernel(arrived, pivot, out):
    total = arrived[0]
    for r in range(1, arrived.shape[0]):
        total = total + arrived[r]
    width = out.shape[1]
    out[0:8, :] = pivot[0:8, :] - total[:, 0:width]
    out[8:16, :] = pivot[8:16, :] - total[:, width : 2 * width]


def call(kernel, shapes, specs, flops=0, moved=0, aliases=None):
    return pl.pallas_call(
        kernel,
        out_shape=shapes,
        in_specs=specs,
        out_specs=jax.tree.map(lambda _: VMEM, shapes),
        compiler_params=PARAMS,
        input_output_aliases=aliases or {},
        cost_estimate=pl.CostEstimate(flops=flops, bytes_accessed=moved, transcendentals=0),
    )


def f32(*shape):
    return jax.ShapeDtypeStruct(shape, jnp.float32)


def on_device(ancestor_inverse, panel, unit_inverse, pivot_inverse, panel_blocks):
    chip = lax.axis_index(CHIPS)
    core = lax.axis_index("core")
    col = lax.axis_index(COL)
    cols = lax.axis_size(COL)
    chips = lax.axis_size(CHIPS)
    rows_here, cols_here = ancestor_inverse.shape
    unit_rows, width = unit_inverse.shape
    range_blocks = cols_here // BLK
    row_blocks = rows_here // BLK
    span = SLOTS * BLK
    total_blocks = panel_blocks.shape[0]

    owner = panel_blocks // range_blocks
    order = jnp.arange(total_blocks, dtype=jnp.int32)
    same = (owner[:, None] == owner[None, :]) & (order[None, :] < order[:, None])
    slot_of = owner * SLOTS + jnp.sum(same.astype(jnp.int32), axis=1)
    all_slots = jnp.arange(cols * SLOTS, dtype=jnp.int32)
    hit = (slot_of[None, :] == all_slots[:, None]).astype(jnp.int32)
    slots = jnp.sum(hit * (order + 1)[None, :], axis=1) - 1
    window = jnp.sum(hit * (panel_blocks + 1)[None, :], axis=1) - 1
    col_blocks = lax.dynamic_slice(window, (col * SLOTS,), (SLOTS,)) - col * range_blocks
    own_blocks = lax.dynamic_slice(window, (chip * SLOTS,), (SLOTS,))
    own_blocks = own_blocks - chip * range_blocks - core * row_blocks
    own_blocks = jnp.where(own_blocks < row_blocks, own_blocks, -1)
    x_lo = lax.axis_index("x_lo")
    place = jnp.stack([col, x_lo]).astype(jnp.int32)
    swap = [(0, 1), (1, 0)]
    half = unit_rows // 2
    lanes = 3 * span + 2 * width

    stored = call(spread_kernel, f32(cols, panel.shape[1], panel.shape[0]), [VMEM])(panel.T)
    stored = lax.all_to_all(stored, COL, 0, 0, tiled=True)
    before = call(unit_kernel, f32(chips, half, lanes), [VMEM])(unit_inverse)
    payload = call(
        pack_kernel,
        f32(chips, half, lanes),
        [SMEM, SMEM, VMEM, VMEM],
        moved=1024 * 1024,
        aliases={3: 0},
    )(slots, place, stored, before)
    gathered = lax.all_to_all(payload, CHIPS, 0, 0, tiled=True)
    gathered = gathered.reshape(chips * half, lanes)
    inverse = call(
        inverse_kernel,
        jax.ShapeDtypeStruct((3 * span, rows_here), jnp.bfloat16),
        [SMEM, VMEM],
        moved=3 * 1024 * 1024,
    )(col_blocks, ancestor_inverse)
    flops = 2 * 3 * chips * unit_rows * width * span
    col_own = call(normal_kernel, f32(width, span), [VMEM], flops, 2 * 1024 * 1024)(gathered)
    col_other = lax.ppermute(col_own, "core", swap)
    partial_tile = call(
        window_kernel,
        f32(width, rows_here),
        [VMEM, VMEM, VMEM],
        flops=2 * 3 * width * span * rows_here,
        moved=3 * 1024 * 1024,
    )(inverse, col_own, col_other)
    half_own = gathered[:, 2 * span : 3 * span]
    partial_tile, half_own = lax.optimization_barrier((partial_tile, half_own))
    half_other = lax.ppermute(half_own, "x_lo", swap)
    row_own = call(
        row_normal_kernel, f32(width, span), [SMEM, VMEM, VMEM, VMEM], flops, 2 * 1024 * 1024
    )(place, gathered, half_own, half_other)
    row_other = lax.ppermute(row_own, "core", swap)
    row_normal = call(
        row_sum_kernel, jax.ShapeDtypeStruct((width, 3 * span), jnp.bfloat16), [VMEM, VMEM]
    )(row_own, row_other)
    partial_tile = partial_tile.reshape(cols, width // cols, rows_here)
    arrived = lax.all_to_all(partial_tile, COL, 0, 0, tiled=True)
    row_count = lax.axis_size(ROW)
    inverse_tile, share = call(
        diagonal_kernel,
        (f32(width // cols, rows_here), f32(row_count, 8, 128)),
        [SMEM, VMEM, VMEM],
        flops=2 * 3 * width * span * (width // cols),
        moved=3 * 1024 * 1024,
    )(own_blocks, row_normal, arrived)
    shares = lax.all_to_all(share, ROW, 0, 0, tiled=True)
    diagonal_block = call(
        final_kernel, f32(*pivot_inverse.shape), [VMEM, VMEM], moved=1024 * 128
    )(shares, pivot_inverse)
    return (inverse_tile, diagonal_block)


def solution(mesh):
    finer = Mesh(
        mesh.devices.reshape(2, mesh.shape["row"] // 4, 2, mesh.shape["col"] // 2, 2),
        (*ROW, *COL),
    )
    return jax.shard_map(
        on_device,
        mesh=finer,
        in_specs=(P(ROW, COL), P(COL, ROW), P(ROW, None), P(ROW, COL), P()),
        out_specs=(P(COL, ROW), P(ROW, COL)),
        check_vma=False,
    )
```

```python
import jax
import jax.numpy as jnp
from jax import lax
from jax.experimental import pallas as pl
from jax.experimental.pallas import tpu as pltpu
from jax.sharding import Mesh
from jax.sharding import PartitionSpec as P

BLK = 128
SLOTS = 3
ROW = ("x_hi", "z", "core")
CHIPS = ("x_hi", "z")
COL = ("y", "x_lo")
PARAMS = pltpu.CompilerParams(vmem_limit_bytes=12 * 1024 * 1024)
VMEM = pl.BlockSpec(memory_space=pltpu.VMEM)
SMEM = pl.BlockSpec(memory_space=pltpu.SMEM)
ANY = pl.BlockSpec(memory_space=pl.ANY)
STEPS = 4


def split(value):
    high = value.astype(jnp.bfloat16)
    low = (value - high.astype(jnp.float32)).astype(jnp.bfloat16)
    return high, low


def left_parts(value):
    high, low = split(value)
    return jnp.concatenate([high, high, low], axis=1)


def right_parts(value):
    high, low = split(value)
    return jnp.concatenate([high, low, high], axis=0)


def dot(left, right):
    return jnp.dot(left, right, preferred_element_type=jnp.float32)


def spread_kernel(panel, out, sems):
    copies = [pltpu.make_async_copy(panel, out.at[col], sems.at[col]) for col in range(out.shape[0])]
    for copy in copies:
        copy.start()
    for copy in copies:
        copy.wait()


def unit_kernel(place, unit, tail, out):
    rows, width = unit.shape
    half = rows // 2
    quarter = width // 4
    start = out.shape[2] - 6 * quarter
    own = unit[...]
    third = jnp.where(place[2] == 0, tail[...], own[:, 2 * quarter : 3 * quarter])
    value = jnp.concatenate([own[:, : 2 * quarter], third], axis=1)
    for chip in range(out.shape[0]):
        out[chip, :, start : start + 3 * quarter] = value[:half]
        out[chip, :, start + 3 * quarter :] = value[half:]


def pack_kernel(slots, place, stored, before, out):
    del before
    here, half = place[0], place[1]
    chips = out.shape[0]
    rows = stored.shape[1] // 2
    span = SLOTS * BLK

    def block(slot, start):
        index = slots[slot]
        safe = jnp.maximum(index, 0)
        lane = pl.multiple_of(lax.rem(safe, 2) * BLK, BLK)
        value = stored[lax.div(safe, 2), pl.ds(start, rows), pl.ds(lane, BLK)]
        return jnp.where(index >= 0, value, 0.0)

    mine = [block(here * SLOTS + s, part * rows) for part in range(2) for s in range(SLOTS)]
    mine = jnp.concatenate(mine, axis=1)
    start = pl.multiple_of(half * rows, rows)
    for chip in range(chips):
        out[chip, :, : 2 * span] = mine
        for s in range(SLOTS):
            at = 2 * span + s * BLK
            out[chip, :, at : at + BLK] = block(chip * SLOTS + s, start)


def unit_parts(gathered, width):
    quarter = width // 4
    start = gathered.shape[1] - 6 * quarter
    middle = gathered.shape[0] // 2
    zeros = jnp.zeros((middle, 2 * quarter), jnp.float32)
    pieces = []
    for at in (start, start + 3 * quarter):
        pieces.append(jnp.concatenate([gathered[:middle, at : at + 2 * quarter], zeros], axis=1))
        ends = gathered[:middle, at + 2 * quarter : at + 3 * quarter]
        pieces.append(jnp.concatenate([gathered[middle:, at : at + 3 * quarter], ends], axis=1))
    return left_parts(jnp.concatenate(pieces, axis=0).T)


def inverse_kernel(blocks, inverse, out):
    listed = []
    for s in range(SLOTS):
        lane = pl.multiple_of(jnp.maximum(blocks[s], 0) * BLK, BLK)
        listed.append(inverse[:, pl.ds(lane, BLK)].T)
    out[...] = right_parts(jnp.concatenate(listed, axis=0))


def normal_kernel(gathered, out):
    width, span = out.shape
    listed = jnp.concatenate([gathered[:, :span], gathered[:, span : 2 * span]], axis=0)
    out[...] = dot(unit_parts(gathered, width), right_parts(listed))


def row_normal_kernel(place, gathered, own, other, out):
    first = place[1] == 0
    low = jnp.where(first, own[...], other[...])
    high = jnp.where(first, other[...], own[...])
    listed = jnp.concatenate([low, high], axis=0)
    out[...] = dot(unit_parts(gathered, out.shape[0]), right_parts(listed))


def row_sum_kernel(own, other, out):
    out[...] = left_parts(own[...] + other[...])


def window_kernel(inverse, own, other, out, made, leave):
    steps = made.shape[0]
    rows = made.shape[1]
    copies = []
    for t in range(steps):
        at = slice(t * rows, (t + 1) * rows)
        made[t] = dot(left_parts(own[at] + other[at]), inverse[...])
        copies.append(pltpu.make_async_copy(made.at[t], out.at[at], leave.at[t]))
        copies[t].start()
    for copy in copies:
        copy.wait()


def diagonal_kernel(blocks, normal, arrived, tile_out, out):
    tile = arrived[0]
    for c in range(1, arrived.shape[0]):
        tile = tile + arrived[c]
    tile_out[...] = -tile
    listed = []
    for s in range(SLOTS):
        place = blocks[s]
        lane = pl.multiple_of(jnp.maximum(place, 0) * BLK, BLK)
        listed.append(jnp.where(place >= 0, tile_out[:, pl.ds(lane, BLK)], 0.0).T)
    total = dot(normal[...], right_parts(jnp.concatenate(listed, axis=0)))
    rows = out.shape[0]
    width = total.shape[1]
    total = total.reshape(rows, 2, 8, width)
    pad = jnp.zeros((rows, 8, 128 - 2 * width), jnp.float32)
    out[...] = jnp.concatenate([total[:, 0], total[:, 1], pad], axis=2)


def final_kernel(arrived, pivot, out):
    total = arrived[0]
    for r in range(1, arrived.shape[0]):
        total = total + arrived[r]
    width = out.shape[1]
    out[0:8, :] = pivot[0:8, :] - total[:, 0:width]
    out[8:16, :] = pivot[8:16, :] - total[:, width : 2 * width]


def call(kernel, shapes, specs, flops=0, moved=0, aliases=None, outs=VMEM, scratch=()):
    return pl.pallas_call(
        kernel,
        out_shape=shapes,
        in_specs=specs,
        out_specs=jax.tree.map(lambda _: outs, shapes),
        scratch_shapes=scratch,
        compiler_params=PARAMS,
        input_output_aliases=aliases or {},
        cost_estimate=pl.CostEstimate(flops=flops, bytes_accessed=moved, transcendentals=0),
    )


def f32(*shape):
    return jax.ShapeDtypeStruct(shape, jnp.float32)


def on_device(ancestor_inverse, panel, unit_inverse, pivot_inverse, panel_blocks):
    chip = lax.axis_index(CHIPS)
    core = lax.axis_index("core")
    col = lax.axis_index(COL)
    cols = lax.axis_size(COL)
    chips = lax.axis_size(CHIPS)
    rows_here, cols_here = ancestor_inverse.shape
    unit_rows, width = unit_inverse.shape
    range_blocks = cols_here // BLK
    row_blocks = rows_here // BLK
    span = SLOTS * BLK
    total_blocks = panel_blocks.shape[0]

    owner = panel_blocks // range_blocks
    order = jnp.arange(total_blocks, dtype=jnp.int32)
    same = (owner[:, None] == owner[None, :]) & (order[None, :] < order[:, None])
    slot_of = owner * SLOTS + jnp.sum(same.astype(jnp.int32), axis=1)
    all_slots = jnp.arange(cols * SLOTS, dtype=jnp.int32)
    hit = (slot_of[None, :] == all_slots[:, None]).astype(jnp.int32)
    slots = jnp.sum(hit * (order + 1)[None, :], axis=1) - 1
    window = jnp.sum(hit * (panel_blocks + 1)[None, :], axis=1) - 1
    col_blocks = lax.dynamic_slice(window, (col * SLOTS,), (SLOTS,)) - col * range_blocks
    own_blocks = lax.dynamic_slice(window, (chip * SLOTS,), (SLOTS,))
    own_blocks = own_blocks - chip * range_blocks - core * row_blocks
    own_blocks = jnp.where(own_blocks < row_blocks, own_blocks, -1)
    x_lo = lax.axis_index("x_lo")
    x_hi = lax.axis_index("x_hi")
    place = jnp.stack([col, x_lo, x_hi]).astype(jnp.int32)
    swap = [(0, 1), (1, 0)]
    half = unit_rows // 2
    lanes = 3 * span + 3 * width // 2

    stored = call(
        spread_kernel,
        f32(cols, panel.shape[1], panel.shape[0]),
        [ANY],
        outs=ANY,
        scratch=[pltpu.SemaphoreType.DMA((cols,))],
    )(panel.T)
    stored = lax.all_to_all(stored, COL, 0, 0, tiled=True)
    tail, slots = lax.optimization_barrier((unit_inverse[:, 3 * width // 4 :], slots))
    tail = lax.ppermute(tail, "x_hi", [(1, 0)])
    before = call(unit_kernel, f32(chips, half, lanes), [SMEM, VMEM, VMEM])(place, unit_inverse, tail)
    inverse = call(
        inverse_kernel,
        jax.ShapeDtypeStruct((3 * span, rows_here), jnp.bfloat16),
        [SMEM, VMEM],
        moved=3 * 1024 * 1024,
    )(col_blocks, ancestor_inverse)
    stored, inverse = lax.optimization_barrier((stored, inverse))
    payload = call(
        pack_kernel,
        f32(chips, half, lanes),
        [SMEM, SMEM, VMEM, VMEM],
        moved=1024 * 1024,
        aliases={3: 0},
    )(slots, place, stored, before)
    gathered = lax.all_to_all(payload, CHIPS, 0, 0, tiled=True)
    gathered = gathered.reshape(chips * half, lanes)
    flops = 2 * 3 * chips * unit_rows * width * span
    col_own = call(normal_kernel, f32(width, span), [VMEM], flops, 2 * 1024 * 1024)(gathered)
    col_other = lax.ppermute(col_own, "core", swap)
    step = (STEPS, width // STEPS, rows_here)
    partial_tile = call(
        window_kernel,
        f32(width, rows_here),
        [VMEM, VMEM, VMEM],
        flops=2 * 3 * width * span * rows_here,
        moved=3 * 1024 * 1024,
        outs=ANY,
        scratch=[
            pltpu.VMEM(step, jnp.float32),
            pltpu.SemaphoreType.DMA((STEPS,)),
        ],
    )(inverse, col_own, col_other)
    half_own = gathered[:, 2 * span : 3 * span]
    partial_tile, half_own = lax.optimization_barrier((partial_tile, half_own))
    half_other = lax.ppermute(half_own, "x_lo", swap)
    row_own = call(
        row_normal_kernel, f32(width, span), [SMEM, VMEM, VMEM, VMEM], flops, 2 * 1024 * 1024
    )(place, gathered, half_own, half_other)
    row_other = lax.ppermute(row_own, "core", swap)
    row_normal = call(
        row_sum_kernel, jax.ShapeDtypeStruct((width, 3 * span), jnp.bfloat16), [VMEM, VMEM]
    )(row_own, row_other)
    partial_tile = partial_tile.reshape(cols, width // cols, rows_here)
    arrived = lax.all_to_all(partial_tile, COL, 0, 0, tiled=True)
    row_count = lax.axis_size(ROW)
    inverse_tile, share = call(
        diagonal_kernel,
        (f32(width // cols, rows_here), f32(row_count, 8, 128)),
        [SMEM, VMEM, VMEM],
        flops=2 * 3 * width * span * (width // cols),
        moved=3 * 1024 * 1024,
    )(own_blocks, row_normal, arrived)
    shares = lax.all_to_all(share, ROW, 0, 0, tiled=True)
    diagonal_block = call(
        final_kernel, f32(*pivot_inverse.shape), [VMEM, VMEM], moved=1024 * 128
    )(shares, pivot_inverse)
    return (inverse_tile, diagonal_block)


def solution(mesh):
    finer = Mesh(
        mesh.devices.reshape(2, mesh.shape["row"] // 4, 2, mesh.shape["col"] // 2, 2),
        (*ROW, *COL),
    )
    return jax.shard_map(
        on_device,
        mesh=finer,
        in_specs=(P(ROW, COL), P(COL, ROW), P(ROW, None), P(ROW, COL), P()),
        out_specs=(P(COL, ROW), P(ROW, COL)),
        check_vma=False,
    )
```

```python
import jax
import jax.numpy as jnp
from jax import lax
from jax.experimental import pallas as pl
from jax.experimental.pallas import tpu as pltpu
from jax.sharding import Mesh
from jax.sharding import PartitionSpec as P

BLK = 128
SLOTS = 3
ROW = ("x_hi", "z", "core")
CHIPS = ("x_hi", "z")
COL = ("y", "x_lo")
SMALL = 12 * 1024 * 1024
LARGE = 56 * 1024 * 1024
VMEM = pl.BlockSpec(memory_space=pltpu.VMEM)
SMEM = pl.BlockSpec(memory_space=pltpu.SMEM)
ANY = pl.BlockSpec(memory_space=pl.ANY)
STEPS = 4
SHARE_ROWS = 16
SHARE_PARTS = 4


def split(value):
    high = value.astype(jnp.bfloat16)
    low = (value - high.astype(jnp.float32)).astype(jnp.bfloat16)
    return high, low


def left_parts(value):
    high, low = split(value)
    return jnp.concatenate([high, high, low], axis=1)


def right_parts(value):
    high, low = split(value)
    return jnp.concatenate([high, low, high], axis=0)


def dot(left, right):
    return jnp.dot(left, right, preferred_element_type=jnp.float32)


def spread_kernel(panel, out, sems):
    copies = [pltpu.make_async_copy(panel, out.at[col], sems.at[col]) for col in range(out.shape[0])]
    for copy in copies:
        copy.start()
    for copy in copies:
        copy.wait()


def unit_kernel(place, unit, far, out):
    rows, width = unit.shape
    half = rows // 2
    quarter = width // 4
    kept = 5 * quarter // 2
    group = place[2]
    own = unit[...]
    other = far[...]
    first = jnp.concatenate([own[:, :quarter], other[:, kept:]], axis=1)
    second = jnp.concatenate([own[:, : 2 * quarter], other[:, kept : 3 * quarter]], axis=1)
    value = jnp.where(group == 0, first, jnp.where(group == 1, second, own[:, :kept]))
    value = jnp.concatenate([value[:half], value[half:]], axis=1)
    start = out.shape[2] - 2 * kept
    for chip in range(out.shape[0]):
        out[chip, :, start:] = value


def pack_kernel(slots, place, stored, before, out):
    del before
    here, half = place[0], place[1]
    chips = out.shape[0]
    rows = stored.shape[1] // 2
    span = SLOTS * BLK

    def block(slot, start):
        index = slots[slot]
        safe = jnp.maximum(index, 0)
        lane = pl.multiple_of(lax.rem(safe, 2) * BLK, BLK)
        value = stored[lax.div(safe, 2), pl.ds(start, rows), pl.ds(lane, BLK)]
        return jnp.where(index >= 0, value, 0.0)

    mine = [block(here * SLOTS + s, part * rows) for part in range(2) for s in range(SLOTS)]
    mine = jnp.concatenate(mine, axis=1)
    start = pl.multiple_of(half * rows, rows)
    for chip in range(chips):
        out[chip, :, : 2 * span] = mine
        for s in range(SLOTS):
            at = 2 * span + s * BLK
            out[chip, :, at : at + BLK] = block(chip * SLOTS + s, start)


def unit_parts(gathered, width):
    quarter = width // 4
    kept = 5 * quarter // 2
    both = gathered[:, gathered.shape[1] - 2 * kept :]
    count = both.shape[0] // 4

    def zeros(lanes):
        return jnp.zeros((count, lanes), jnp.float32)

    pieces = []
    for value in (both[:, :kept], both[:, kept:]):
        g0, g1, g2, g3 = (value[g * count : (g + 1) * count] for g in range(4))
        pieces.append(jnp.concatenate([g0[:, :quarter], zeros(3 * quarter)], axis=1))
        pieces.append(jnp.concatenate([g1[:, : 2 * quarter], zeros(2 * quarter)], axis=1))
        pieces.append(jnp.concatenate([g2, g1[:, 2 * quarter :], zeros(quarter)], axis=1))
        pieces.append(jnp.concatenate([g3, g0[:, quarter:]], axis=1))
    return left_parts(jnp.concatenate(pieces, axis=0).T)


def inverse_kernel(blocks, inverse, out, held, sems):
    copies = []
    for s in range(SLOTS):
        lane = pl.multiple_of(jnp.maximum(blocks[s], 0) * BLK, BLK)
        copies.append(pltpu.make_async_copy(inverse.at[:, pl.ds(lane, BLK)], held.at[s], sems.at[s]))
    for copy in copies:
        copy.start()
    span = SLOTS * BLK
    for s in range(SLOTS):
        copies[s].wait()
        high, low = split(held[s].T)
        for part, value in enumerate((high, low, high)):
            out[part * span + s * BLK : part * span + (s + 1) * BLK, :] = value


def normal_kernel(gathered, out):
    width, span = out.shape
    listed = jnp.concatenate([gathered[:, :span], gathered[:, span : 2 * span]], axis=0)
    out[...] = dot(unit_parts(gathered, width), right_parts(listed))


def row_normal_kernel(place, gathered, own, other, out):
    first = place[1] == 0
    low = jnp.where(first, own[...], other[...])
    high = jnp.where(first, other[...], own[...])
    listed = jnp.concatenate([low, high], axis=0)
    out[...] = dot(unit_parts(gathered, out.shape[0]), right_parts(listed))


def row_sum_kernel(own, other, out, total, ordered):
    width = own.shape[0]
    count = width // SHARE_ROWS
    each = SHARE_ROWS // SHARE_PARTS
    for s in range(SLOTS):
        at = slice(s * BLK, (s + 1) * BLK)
        total[s] = own[:, at] + other[:, at]
        for row in range(SHARE_ROWS):
            part, place = row // each, row % each
            value = total[s, pl.ds(row, count, stride=SHARE_ROWS), :]
            ordered[s, pl.ds(part * count * each + place, count, stride=each), :] = value
    out[...] = left_parts(jnp.concatenate([ordered[s] for s in range(SLOTS)], axis=1))


def window_kernel(inverse, own, other, out, made, leave):
    steps = made.shape[0]
    rows = made.shape[1]
    copies = []
    for t in range(steps):
        at = slice(t * rows, (t + 1) * rows)
        made[t] = dot(left_parts(own[at] + other[at]), inverse[...])
        copies.append(pltpu.make_async_copy(made.at[t], out.at[at], leave.at[t]))
        copies[t].start()
    for copy in copies:
        copy.wait()


def diagonal_kernel(blocks, normal, arrived, tile_out, out):
    tile = arrived[0]
    for c in range(1, arrived.shape[0]):
        tile = tile + arrived[c]
    tile_out[...] = -tile
    listed = []
    for s in range(SLOTS):
        place = blocks[s]
        lane = pl.multiple_of(jnp.maximum(place, 0) * BLK, BLK)
        listed.append(jnp.where(place >= 0, tile_out[:, pl.ds(lane, BLK)], 0.0).T)
    total = dot(normal[...], right_parts(jnp.concatenate(listed, axis=0)))
    rows = out.shape[0]
    out[...] = jnp.concatenate([total[p * rows : (p + 1) * rows] for p in range(SHARE_PARTS)], axis=1)


def final_kernel(arrived, pivot, out):
    total = arrived[0]
    for r in range(1, arrived.shape[0]):
        total = total + arrived[r]
    rows, width = total.shape[0], out.shape[1]
    for p in range(SHARE_PARTS):
        at = slice(p * rows, (p + 1) * rows)
        out[at, :] = pivot[at, :] - total[:, p * width : (p + 1) * width]


def call(kernel, shapes, specs, flops=0, moved=0, aliases=None, outs=VMEM, scratch=(), limit=SMALL):
    return pl.pallas_call(
        kernel,
        out_shape=shapes,
        in_specs=specs,
        out_specs=jax.tree.map(lambda _: outs, shapes),
        scratch_shapes=scratch,
        compiler_params=pltpu.CompilerParams(vmem_limit_bytes=limit),
        input_output_aliases=aliases or {},
        cost_estimate=pl.CostEstimate(flops=flops, bytes_accessed=moved, transcendentals=0),
    )


def f32(*shape):
    return jax.ShapeDtypeStruct(shape, jnp.float32)


def on_device(ancestor_inverse, panel, unit_inverse, pivot_inverse, panel_blocks):
    chip = lax.axis_index(CHIPS)
    core = lax.axis_index("core")
    col = lax.axis_index(COL)
    cols = lax.axis_size(COL)
    chips = lax.axis_size(CHIPS)
    rows_here, cols_here = ancestor_inverse.shape
    unit_rows, width = unit_inverse.shape
    range_blocks = cols_here // BLK
    row_blocks = rows_here // BLK
    span = SLOTS * BLK
    total_blocks = panel_blocks.shape[0]

    owner = panel_blocks // range_blocks
    order = jnp.arange(total_blocks, dtype=jnp.int32)
    same = (owner[:, None] == owner[None, :]) & (order[None, :] < order[:, None])
    slot_of = owner * SLOTS + jnp.sum(same.astype(jnp.int32), axis=1)
    all_slots = jnp.arange(cols * SLOTS, dtype=jnp.int32)
    hit = (slot_of[None, :] == all_slots[:, None]).astype(jnp.int32)
    slots = jnp.sum(hit * (order + 1)[None, :], axis=1) - 1
    window = jnp.sum(hit * (panel_blocks + 1)[None, :], axis=1) - 1
    col_blocks = lax.dynamic_slice(window, (col * SLOTS,), (SLOTS,)) - col * range_blocks
    own_blocks = lax.dynamic_slice(window, (chip * SLOTS,), (SLOTS,))
    own_blocks = own_blocks - chip * range_blocks - core * row_blocks
    own_blocks = jnp.where(own_blocks < row_blocks, own_blocks, -1)
    x_lo = lax.axis_index("x_lo")
    heights = lax.axis_size("z")
    group = chip // (heights // 2)
    place = jnp.stack([col, x_lo, group]).astype(jnp.int32)
    swap = [(0, 1), (1, 0)]
    half = unit_rows // 2
    lanes = 3 * span + 5 * width // 4

    stored = call(
        spread_kernel,
        f32(cols, panel.shape[1], panel.shape[0]),
        [ANY],
        outs=ANY,
        scratch=[pltpu.SemaphoreType.DMA((cols,))],
        limit=LARGE,
    )(panel.T)
    stored = lax.all_to_all(stored, COL, 0, 0, tiled=True)
    unit, slots = lax.optimization_barrier((unit_inverse, slots))
    across = [(heights + z, z ^ (heights // 2)) for z in range(heights)]
    far = lax.ppermute(unit, CHIPS, across)
    before = call(unit_kernel, f32(chips, half, lanes), [SMEM, VMEM, VMEM])(place, unit, far)
    inverse = call(
        inverse_kernel,
        jax.ShapeDtypeStruct((3 * span, rows_here), jnp.bfloat16),
        [SMEM, ANY],
        moved=3 * 1024 * 1024,
        scratch=[pltpu.VMEM((SLOTS, rows_here, BLK), jnp.float32), pltpu.SemaphoreType.DMA((SLOTS,))],
        limit=LARGE,
    )(col_blocks, ancestor_inverse)
    stored, inverse = lax.optimization_barrier((stored, inverse))
    payload = call(
        pack_kernel,
        f32(chips, half, lanes),
        [SMEM, SMEM, VMEM, VMEM],
        moved=1024 * 1024,
        aliases={3: 0},
    )(slots, place, stored, before)
    gathered = lax.all_to_all(payload, CHIPS, 0, 0, tiled=True)
    gathered = gathered.reshape(chips * half, lanes)
    flops = 2 * 3 * chips * unit_rows * width * span
    col_own = call(normal_kernel, f32(width, span), [VMEM], flops, 2 * 1024 * 1024)(gathered)
    col_other = lax.ppermute(col_own, "core", swap)
    step = (STEPS, width // STEPS, rows_here)
    partial_tile = call(
        window_kernel,
        f32(width, rows_here),
        [VMEM, VMEM, VMEM],
        flops=2 * 3 * width * span * rows_here,
        moved=3 * 1024 * 1024,
        outs=ANY,
        scratch=[
            pltpu.VMEM(step, jnp.float32),
            pltpu.SemaphoreType.DMA((STEPS,)),
        ],
    )(inverse, col_own, col_other)
    half_own = gathered[:, 2 * span : 3 * span]
    partial_tile, half_own = lax.optimization_barrier((partial_tile, half_own))
    half_other = lax.ppermute(half_own, "x_lo", swap)
    row_own = call(
        row_normal_kernel, f32(width, span), [SMEM, VMEM, VMEM, VMEM], flops, 2 * 1024 * 1024
    )(place, gathered, half_own, half_other)
    row_other = lax.ppermute(row_own, "core", swap)
    row_normal = call(
        row_sum_kernel,
        jax.ShapeDtypeStruct((width, 3 * span), jnp.bfloat16),
        [VMEM, VMEM],
        scratch=[pltpu.VMEM((SLOTS, width, BLK), jnp.float32)] * 2,
    )(row_own, row_other)
    partial_tile = partial_tile.reshape(cols, width // cols, rows_here)
    arrived = lax.all_to_all(partial_tile, COL, 0, 0, tiled=True)
    row_count = lax.axis_size(ROW)
    inverse_tile, share = call(
        diagonal_kernel,
        (f32(width // cols, rows_here), f32(width // SHARE_PARTS, BLK)),
        [SMEM, VMEM, VMEM],
        flops=2 * 3 * width * span * (width // cols),
        moved=3 * 1024 * 1024,
    )(own_blocks, row_normal, arrived)
    share = share.reshape(row_count, -1, BLK)
    shares = lax.all_to_all(share, ROW, 0, 0, tiled=True)
    diagonal_block = call(
        final_kernel, f32(*pivot_inverse.shape), [VMEM, VMEM], moved=1024 * 128
    )(shares, pivot_inverse)
    return (inverse_tile, diagonal_block)


def solution(mesh):
    finer = Mesh(
        mesh.devices.reshape(2, mesh.shape["row"] // 4, 2, mesh.shape["col"] // 2, 2),
        (*ROW, *COL),
    )
    return jax.shard_map(
        on_device,
        mesh=finer,
        in_specs=(P(ROW, COL), P(COL, ROW), P(ROW, None), P(ROW, COL), P()),
        out_specs=(P(COL, ROW), P(ROW, COL)),
        check_vma=False,
    )
```

```python
import jax
import jax.numpy as jnp
from jax import lax
from jax.experimental import pallas as pl
from jax.experimental.pallas import tpu as pltpu
from jax.sharding import Mesh
from jax.sharding import PartitionSpec as P

BLK = 128
SLOTS = 3
ROW = ("x_hi", "z", "core")
CHIPS = ("x_hi", "z")
COL = ("y", "x_lo")
LIMIT = 12 * 1024 * 1024
VMEM = pl.BlockSpec(memory_space=pltpu.VMEM)
SMEM = pl.BlockSpec(memory_space=pltpu.SMEM)
ANY = pl.BlockSpec(memory_space=pl.ANY)
STEPS = 4
SHARE_ROWS = 16
SHARE_PARTS = 4


def split(value):
    high = value.astype(jnp.bfloat16)
    low = (value - high.astype(jnp.float32)).astype(jnp.bfloat16)
    return high, low


def left_parts(value):
    high, low = split(value)
    return jnp.concatenate([high, high, low], axis=1)


def right_parts(value):
    high, low = split(value)
    return jnp.concatenate([high, low, high], axis=0)


def dot(left, right):
    return jnp.dot(left, right, preferred_element_type=jnp.float32)


def spread_kernel(panel, out, sems):
    copies = [pltpu.make_async_copy(panel, out.at[col], sems.at[col]) for col in range(out.shape[0])]
    for copy in copies:
        copy.start()
    for copy in copies:
        copy.wait()


def unit_kernel(place, unit, far, out):
    rows, width = unit.shape
    half = rows // 2
    quarter = width // 4
    kept = 5 * quarter // 2
    group = place[2]
    own = unit[...]
    other = far[...]
    first = jnp.concatenate([own[:, :quarter], other[:, kept:]], axis=1)
    second = jnp.concatenate([own[:, : 2 * quarter], other[:, kept : 3 * quarter]], axis=1)
    value = jnp.where(group == 0, first, jnp.where(group == 1, second, own[:, :kept]))
    value = jnp.concatenate([value[:half], value[half:]], axis=1)
    start = out.shape[2] - 2 * kept
    for chip in range(out.shape[0]):
        out[chip, :, start:] = value


def pack_kernel(slots, place, stored, before, out):
    del before
    here, half = place[0], place[1]
    chips = out.shape[0]
    rows = stored.shape[1] // 2
    span = SLOTS * BLK

    def block(slot, start):
        index = slots[slot]
        safe = jnp.maximum(index, 0)
        lane = pl.multiple_of(lax.rem(safe, 2) * BLK, BLK)
        value = stored[lax.div(safe, 2), pl.ds(start, rows), pl.ds(lane, BLK)]
        return jnp.where(index >= 0, value, 0.0)

    mine = [block(here * SLOTS + s, part * rows) for part in range(2) for s in range(SLOTS)]
    mine = jnp.concatenate(mine, axis=1)
    start = pl.multiple_of(half * rows, rows)
    for chip in range(chips):
        out[chip, :, : 2 * span] = mine
        for s in range(SLOTS):
            at = 2 * span + s * BLK
            out[chip, :, at : at + BLK] = block(chip * SLOTS + s, start)


def unit_parts(gathered, width):
    quarter = width // 4
    kept = 5 * quarter // 2
    both = gathered[:, gathered.shape[1] - 2 * kept :]
    count = both.shape[0] // 4

    def zeros(lanes):
        return jnp.zeros((count, lanes), jnp.float32)

    pieces = []
    for value in (both[:, :kept], both[:, kept:]):
        g0, g1, g2, g3 = (value[g * count : (g + 1) * count] for g in range(4))
        pieces.append(jnp.concatenate([g0[:, :quarter], zeros(3 * quarter)], axis=1))
        pieces.append(jnp.concatenate([g1[:, : 2 * quarter], zeros(2 * quarter)], axis=1))
        pieces.append(jnp.concatenate([g2, g1[:, 2 * quarter :], zeros(quarter)], axis=1))
        pieces.append(jnp.concatenate([g3, g0[:, quarter:]], axis=1))
    return left_parts(jnp.concatenate(pieces, axis=0).T)


def inverse_kernel(blocks, inverse, out):
    listed = []
    for s in range(SLOTS):
        lane = pl.multiple_of(jnp.maximum(blocks[s], 0) * BLK, BLK)
        listed.append(inverse[:, pl.ds(lane, BLK)].T)
    out[...] = right_parts(jnp.concatenate(listed, axis=0))


def normal_kernel(gathered, out):
    width, span = out.shape
    listed = jnp.concatenate([gathered[:, :span], gathered[:, span : 2 * span]], axis=0)
    out[...] = dot(unit_parts(gathered, width), right_parts(listed))


def row_normal_kernel(place, gathered, own, other, out):
    first = place[1] == 0
    low = jnp.where(first, own[...], other[...])
    high = jnp.where(first, other[...], own[...])
    listed = jnp.concatenate([low, high], axis=0)
    out[...] = dot(unit_parts(gathered, out.shape[0]), right_parts(listed))


def row_sum_kernel(own, other, out, total, ordered):
    width = own.shape[0]
    count = width // SHARE_ROWS
    each = SHARE_ROWS // SHARE_PARTS
    for s in range(SLOTS):
        at = slice(s * BLK, (s + 1) * BLK)
        total[s] = own[:, at] + other[:, at]
        for row in range(SHARE_ROWS):
            part, place = row // each, row % each
            value = total[s, pl.ds(row, count, stride=SHARE_ROWS), :]
            ordered[s, pl.ds(part * count * each + place, count, stride=each), :] = value
    out[...] = left_parts(jnp.concatenate([ordered[s] for s in range(SLOTS)], axis=1))


def window_kernel(inverse, own, other, out, made, leave):
    steps = made.shape[0]
    rows = made.shape[1]
    copies = []
    for t in range(steps):
        at = slice(t * rows, (t + 1) * rows)
        made[t] = dot(left_parts(own[at] + other[at]), inverse[...])
        copies.append(pltpu.make_async_copy(made.at[t], out.at[at], leave.at[t]))
        copies[t].start()
    for copy in copies:
        copy.wait()


def diagonal_kernel(blocks, normal, arrived, tile_out, out):
    tile = arrived[0]
    for c in range(1, arrived.shape[0]):
        tile = tile + arrived[c]
    tile_out[...] = -tile
    listed = []
    for s in range(SLOTS):
        place = blocks[s]
        lane = pl.multiple_of(jnp.maximum(place, 0) * BLK, BLK)
        listed.append(jnp.where(place >= 0, tile_out[:, pl.ds(lane, BLK)], 0.0).T)
    total = dot(normal[...], right_parts(jnp.concatenate(listed, axis=0)))
    rows = out.shape[0]
    out[...] = jnp.concatenate([total[p * rows : (p + 1) * rows] for p in range(SHARE_PARTS)], axis=1)


def final_kernel(arrived, pivot, out):
    total = arrived[0]
    for r in range(1, arrived.shape[0]):
        total = total + arrived[r]
    rows, width = total.shape[0], out.shape[1]
    for p in range(SHARE_PARTS):
        at = slice(p * rows, (p + 1) * rows)
        out[at, :] = pivot[at, :] - total[:, p * width : (p + 1) * width]


def call(kernel, shapes, specs, flops=0, moved=0, aliases=None, outs=VMEM, scratch=()):
    return pl.pallas_call(
        kernel,
        out_shape=shapes,
        in_specs=specs,
        out_specs=jax.tree.map(lambda _: outs, shapes),
        scratch_shapes=scratch,
        compiler_params=pltpu.CompilerParams(vmem_limit_bytes=LIMIT),
        input_output_aliases=aliases or {},
        cost_estimate=pl.CostEstimate(flops=flops, bytes_accessed=moved, transcendentals=0),
    )


def f32(*shape):
    return jax.ShapeDtypeStruct(shape, jnp.float32)


def on_device(ancestor_inverse, panel, unit_inverse, pivot_inverse, panel_blocks):
    chip = lax.axis_index(CHIPS)
    core = lax.axis_index("core")
    col = lax.axis_index(COL)
    cols = lax.axis_size(COL)
    chips = lax.axis_size(CHIPS)
    rows_here, cols_here = ancestor_inverse.shape
    unit_rows, width = unit_inverse.shape
    range_blocks = cols_here // BLK
    row_blocks = rows_here // BLK
    span = SLOTS * BLK
    total_blocks = panel_blocks.shape[0]

    owner = panel_blocks // range_blocks
    order = jnp.arange(total_blocks, dtype=jnp.int32)
    same = (owner[:, None] == owner[None, :]) & (order[None, :] < order[:, None])
    slot_of = owner * SLOTS + jnp.sum(same.astype(jnp.int32), axis=1)
    all_slots = jnp.arange(cols * SLOTS, dtype=jnp.int32)
    hit = (slot_of[None, :] == all_slots[:, None]).astype(jnp.int32)
    slots = jnp.sum(hit * (order + 1)[None, :], axis=1) - 1
    window = jnp.sum(hit * (panel_blocks + 1)[None, :], axis=1) - 1
    col_blocks = lax.dynamic_slice(window, (col * SLOTS,), (SLOTS,)) - col * range_blocks
    own_blocks = lax.dynamic_slice(window, (chip * SLOTS,), (SLOTS,))
    own_blocks = own_blocks - chip * range_blocks - core * row_blocks
    own_blocks = jnp.where(own_blocks < row_blocks, own_blocks, -1)
    x_lo = lax.axis_index("x_lo")
    heights = lax.axis_size("z")
    group = chip // (heights // 2)
    place = jnp.stack([col, x_lo, group]).astype(jnp.int32)
    swap = [(0, 1), (1, 0)]
    half = unit_rows // 2
    lanes = 3 * span + 5 * width // 4

    stored = call(
        spread_kernel,
        f32(cols, panel.shape[1], panel.shape[0]),
        [VMEM],
        outs=ANY,
        scratch=[pltpu.SemaphoreType.DMA((cols,))],
    )(panel.T)
    stored = lax.all_to_all(stored, COL, 0, 0, tiled=True)
    unit, slots = lax.optimization_barrier((unit_inverse, slots))
    across = [(heights + z, z ^ (heights // 2)) for z in range(heights)]
    far = lax.ppermute(unit, CHIPS, across)
    before = call(unit_kernel, f32(chips, half, lanes), [SMEM, VMEM, VMEM])(place, unit, far)
    inverse = call(
        inverse_kernel,
        jax.ShapeDtypeStruct((3 * span, rows_here), jnp.bfloat16),
        [SMEM, VMEM],
        moved=3 * 1024 * 1024,
    )(col_blocks, ancestor_inverse)
    stored, inverse = lax.optimization_barrier((stored, inverse))
    payload = call(
        pack_kernel,
        f32(chips, half, lanes),
        [SMEM, SMEM, VMEM, VMEM],
        moved=1024 * 1024,
        aliases={3: 0},
    )(slots, place, stored, before)
    gathered = lax.all_to_all(payload, CHIPS, 0, 0, tiled=True)
    gathered = gathered.reshape(chips * half, lanes)
    flops = 2 * 3 * chips * unit_rows * width * span
    col_own = call(normal_kernel, f32(width, span), [VMEM], flops, 2 * 1024 * 1024)(gathered)
    col_other = lax.ppermute(col_own, "core", swap)
    step = (STEPS, width // STEPS, rows_here)
    partial_tile = call(
        window_kernel,
        f32(width, rows_here),
        [VMEM, VMEM, VMEM],
        flops=2 * 3 * width * span * rows_here,
        moved=3 * 1024 * 1024,
        outs=ANY,
        scratch=[
            pltpu.VMEM(step, jnp.float32),
            pltpu.SemaphoreType.DMA((STEPS,)),
        ],
    )(inverse, col_own, col_other)
    half_own = gathered[:, 2 * span : 3 * span]
    partial_tile, half_own = lax.optimization_barrier((partial_tile, half_own))
    half_other = lax.ppermute(half_own, "x_lo", swap)
    row_own = call(
        row_normal_kernel, f32(width, span), [SMEM, VMEM, VMEM, VMEM], flops, 2 * 1024 * 1024
    )(place, gathered, half_own, half_other)
    row_other = lax.ppermute(row_own, "core", swap)
    row_normal = call(
        row_sum_kernel,
        jax.ShapeDtypeStruct((width, 3 * span), jnp.bfloat16),
        [VMEM, VMEM],
        scratch=[pltpu.VMEM((SLOTS, width, BLK), jnp.float32)] * 2,
    )(row_own, row_other)
    partial_tile = partial_tile.reshape(cols, width // cols, rows_here)
    arrived = lax.all_to_all(partial_tile, COL, 0, 0, tiled=True)
    row_count = lax.axis_size(ROW)
    inverse_tile, share = call(
        diagonal_kernel,
        (f32(width // cols, rows_here), f32(width // SHARE_PARTS, BLK)),
        [SMEM, VMEM, VMEM],
        flops=2 * 3 * width * span * (width // cols),
        moved=3 * 1024 * 1024,
    )(own_blocks, row_normal, arrived)
    share = share.reshape(row_count, -1, BLK)
    shares = lax.all_to_all(share, ROW, 0, 0, tiled=True)
    diagonal_block = call(
        final_kernel, f32(*pivot_inverse.shape), [VMEM, VMEM], moved=1024 * 128
    )(shares, pivot_inverse)
    return (inverse_tile, diagonal_block)


def solution(mesh):
    finer = Mesh(
        mesh.devices.reshape(2, mesh.shape["row"] // 4, 2, mesh.shape["col"] // 2, 2),
        (*ROW, *COL),
    )
    return jax.shard_map(
        on_device,
        mesh=finer,
        in_specs=(P(ROW, COL), P(COL, ROW), P(ROW, None), P(ROW, COL), P()),
        out_specs=(P(COL, ROW), P(ROW, COL)),
        check_vma=False,
    )
```

```python
import jax
import jax.numpy as jnp
from jax import lax
from jax.experimental import pallas as pl
from jax.experimental.pallas import tpu as pltpu
from jax.sharding import Mesh
from jax.sharding import PartitionSpec as P

BLK = 128
SLOTS = 3
ROW = ("x_hi", "z", "core")
CHIPS = ("x_hi", "z")
COL = ("y", "x_lo")
SMALL = 12 * 1024 * 1024
LARGE = 56 * 1024 * 1024
VMEM = pl.BlockSpec(memory_space=pltpu.VMEM)
SMEM = pl.BlockSpec(memory_space=pltpu.SMEM)
ANY = pl.BlockSpec(memory_space=pl.ANY)
STEPS = 4
SHARE_ROWS = 16
SHARE_PARTS = 4


def split(value):
    high = value.astype(jnp.bfloat16)
    low = (value - high.astype(jnp.float32)).astype(jnp.bfloat16)
    return high, low


def left_parts(value):
    high, low = split(value)
    return jnp.concatenate([high, high, low], axis=1)


def right_parts(value):
    high, low = split(value)
    return jnp.concatenate([high, low, high], axis=0)


def dot(left, right):
    return jnp.dot(left, right, preferred_element_type=jnp.float32)


def spread_kernel(panel, out, held, sems):
    first = pltpu.make_async_copy(panel, held, sems.at[0])
    first.start()
    first.wait()
    copies = [pltpu.make_async_copy(held, out.at[col], sems.at[1 + col]) for col in range(out.shape[0])]
    for copy in copies:
        copy.start()
    for copy in copies:
        copy.wait()


def unit_kernel(place, unit, far, out):
    rows, width = unit.shape
    half = rows // 2
    quarter = width // 4
    start = out.shape[2] - 6 * quarter
    third = jnp.where(place[2] == 0, far[:, 3 * quarter :], unit[:, 2 * quarter : 3 * quarter])
    value = jnp.concatenate([unit[:, : 2 * quarter], third], axis=1)
    for chip in range(out.shape[0]):
        out[chip, :, start : start + 3 * quarter] = value[:half]
        out[chip, :, start + 3 * quarter :] = value[half:]


def pack_kernel(slots, place, stored, before, out):
    del before
    here, half = place[0], place[1]
    chips = out.shape[0]
    rows = stored.shape[1] // 2
    span = SLOTS * BLK

    def block(slot, start):
        index = slots[slot]
        safe = jnp.maximum(index, 0)
        lane = pl.multiple_of(lax.rem(safe, 2) * BLK, BLK)
        value = stored[lax.div(safe, 2), pl.ds(start, rows), pl.ds(lane, BLK)]
        return jnp.where(index >= 0, value, 0.0)

    mine = [block(here * SLOTS + s, part * rows) for part in range(2) for s in range(SLOTS)]
    mine = jnp.concatenate(mine, axis=1)
    start = pl.multiple_of(half * rows, rows)
    for chip in range(chips):
        out[chip, :, : 2 * span] = mine
        for s in range(SLOTS):
            at = 2 * span + s * BLK
            out[chip, :, at : at + BLK] = block(chip * SLOTS + s, start)


def unit_parts(gathered, width):
    quarter = width // 4
    start = gathered.shape[1] - 6 * quarter
    middle = gathered.shape[0] // 2
    zeros = jnp.zeros((middle, 2 * quarter), jnp.float32)
    pieces = []
    for at in (start, start + 3 * quarter):
        pieces.append(jnp.concatenate([gathered[:middle, at : at + 2 * quarter], zeros], axis=1))
        ends = gathered[:middle, at + 2 * quarter : at + 3 * quarter]
        pieces.append(jnp.concatenate([gathered[middle:, at : at + 3 * quarter], ends], axis=1))
    return left_parts(jnp.concatenate(pieces, axis=0).T)


def inverse_kernel(blocks, inverse, out):
    listed = []
    for s in range(SLOTS):
        lane = pl.multiple_of(jnp.maximum(blocks[s], 0) * BLK, BLK)
        listed.append(inverse[:, pl.ds(lane, BLK)].T)
    out[...] = right_parts(jnp.concatenate(listed, axis=0))


def normal_kernel(gathered, out):
    width, span = out.shape
    listed = jnp.concatenate([gathered[:, :span], gathered[:, span : 2 * span]], axis=0)
    out[...] = dot(unit_parts(gathered, width), right_parts(listed))


def row_normal_kernel(place, gathered, own, other, out):
    first = place[1] == 0
    low = jnp.where(first, own[...], other[...])
    high = jnp.where(first, other[...], own[...])
    listed = jnp.concatenate([low, high], axis=0)
    out[...] = dot(unit_parts(gathered, out.shape[0]), right_parts(listed))


def row_sum_kernel(own, other, out, total, ordered):
    width = own.shape[0]
    count = width // SHARE_ROWS
    each = SHARE_ROWS // SHARE_PARTS
    for s in range(SLOTS):
        at = slice(s * BLK, (s + 1) * BLK)
        total[s] = own[:, at] + other[:, at]
        for row in range(SHARE_ROWS):
            part, place = row // each, row % each
            value = total[s, pl.ds(row, count, stride=SHARE_ROWS), :]
            ordered[s, pl.ds(part * count * each + place, count, stride=each), :] = value
    out[...] = left_parts(jnp.concatenate([ordered[s] for s in range(SLOTS)], axis=1))


def window_kernel(inverse, own, other, out, made, leave):
    steps = made.shape[0]
    rows = made.shape[1]
    copies = []
    for t in range(steps):
        at = slice(t * rows, (t + 1) * rows)
        made[t] = dot(left_parts(own[at] + other[at]), inverse[...])
        copies.append(pltpu.make_async_copy(made.at[t], out.at[at], leave.at[t]))
        copies[t].start()
    for copy in copies:
        copy.wait()


def diagonal_kernel(blocks, normal, arrived, tile_out, out):
    tile = arrived[0]
    for c in range(1, arrived.shape[0]):
        tile = tile + arrived[c]
    tile_out[...] = -tile
    listed = []
    for s in range(SLOTS):
        place = blocks[s]
        lane = pl.multiple_of(jnp.maximum(place, 0) * BLK, BLK)
        listed.append(jnp.where(place >= 0, tile_out[:, pl.ds(lane, BLK)], 0.0).T)
    total = dot(normal[...], right_parts(jnp.concatenate(listed, axis=0)))
    rows = out.shape[0]
    out[...] = jnp.concatenate([total[p * rows : (p + 1) * rows] for p in range(SHARE_PARTS)], axis=1)


def final_kernel(arrived, pivot, out):
    total = arrived[0]
    for r in range(1, arrived.shape[0]):
        total = total + arrived[r]
    rows, width = total.shape[0], out.shape[1]
    for p in range(SHARE_PARTS):
        at = slice(p * rows, (p + 1) * rows)
        out[at, :] = pivot[at, :] - total[:, p * width : (p + 1) * width]


def call(kernel, shapes, specs, flops=0, moved=0, aliases=None, outs=VMEM, scratch=(), limit=SMALL):
    return pl.pallas_call(
        kernel,
        out_shape=shapes,
        in_specs=specs,
        out_specs=jax.tree.map(lambda _: outs, shapes),
        scratch_shapes=scratch,
        compiler_params=pltpu.CompilerParams(vmem_limit_bytes=limit),
        input_output_aliases=aliases or {},
        cost_estimate=pl.CostEstimate(flops=flops, bytes_accessed=moved, transcendentals=0),
    )


def f32(*shape):
    return jax.ShapeDtypeStruct(shape, jnp.float32)


def on_device(ancestor_inverse, panel, unit_inverse, pivot_inverse, panel_blocks):
    chip = lax.axis_index(CHIPS)
    core = lax.axis_index("core")
    col = lax.axis_index(COL)
    cols = lax.axis_size(COL)
    chips = lax.axis_size(CHIPS)
    rows_here, cols_here = ancestor_inverse.shape
    unit_rows, width = unit_inverse.shape
    range_blocks = cols_here // BLK
    row_blocks = rows_here // BLK
    span = SLOTS * BLK
    total_blocks = panel_blocks.shape[0]

    owner = panel_blocks // range_blocks
    order = jnp.arange(total_blocks, dtype=jnp.int32)
    same = (owner[:, None] == owner[None, :]) & (order[None, :] < order[:, None])
    slot_of = owner * SLOTS + jnp.sum(same.astype(jnp.int32), axis=1)
    all_slots = jnp.arange(cols * SLOTS, dtype=jnp.int32)
    hit = (slot_of[None, :] == all_slots[:, None]).astype(jnp.int32)
    slots = jnp.sum(hit * (order + 1)[None, :], axis=1) - 1
    window = jnp.sum(hit * (panel_blocks + 1)[None, :], axis=1) - 1
    col_blocks = lax.dynamic_slice(window, (col * SLOTS,), (SLOTS,)) - col * range_blocks
    own_blocks = lax.dynamic_slice(window, (chip * SLOTS,), (SLOTS,))
    own_blocks = own_blocks - chip * range_blocks - core * row_blocks
    own_blocks = jnp.where(own_blocks < row_blocks, own_blocks, -1)
    x_lo = lax.axis_index("x_lo")
    x_hi = lax.axis_index("x_hi")
    place = jnp.stack([col, x_lo, x_hi]).astype(jnp.int32)
    swap = [(0, 1), (1, 0)]
    half = unit_rows // 2
    lanes = 3 * span + 3 * width // 2

    stored = call(
        spread_kernel,
        f32(cols, panel.shape[1], panel.shape[0]),
        [ANY],
        outs=ANY,
        scratch=[
            pltpu.VMEM((panel.shape[1], panel.shape[0]), jnp.float32),
            pltpu.SemaphoreType.DMA((1 + cols,)),
        ],
        limit=LARGE,
    )(panel.T)
    stored = lax.all_to_all(stored, COL, 0, 0, tiled=True)
    far = lax.ppermute(unit_inverse, "x_hi", [(1, 0)])
    before = call(unit_kernel, f32(chips, half, lanes), [SMEM, VMEM, VMEM])(place, unit_inverse, far)
    inverse = call(
        inverse_kernel,
        jax.ShapeDtypeStruct((3 * span, rows_here), jnp.bfloat16),
        [SMEM, VMEM],
        moved=3 * 1024 * 1024,
    )(col_blocks, ancestor_inverse)
    stored, inverse = lax.optimization_barrier((stored, inverse))
    payload = call(
        pack_kernel,
        f32(chips, half, lanes),
        [SMEM, SMEM, VMEM, VMEM],
        moved=1024 * 1024,
        aliases={3: 0},
    )(slots, place, stored, before)
    gathered = lax.all_to_all(payload, CHIPS, 0, 0, tiled=True)
    gathered = gathered.reshape(chips * half, lanes)
    flops = 2 * 3 * chips * unit_rows * width * span
    col_own = call(normal_kernel, f32(width, span), [VMEM], flops, 2 * 1024 * 1024)(gathered)
    col_other = lax.ppermute(col_own, "core", swap)
    step = (STEPS, width // STEPS, rows_here)
    partial_tile = call(
        window_kernel,
        f32(width, rows_here),
        [VMEM, VMEM, VMEM],
        flops=2 * 3 * width * span * rows_here,
        moved=3 * 1024 * 1024,
        outs=ANY,
        scratch=[
            pltpu.VMEM(step, jnp.float32),
            pltpu.SemaphoreType.DMA((STEPS,)),
        ],
    )(inverse, col_own, col_other)
    half_own = gathered[:, 2 * span : 3 * span]
    partial_tile, half_own = lax.optimization_barrier((partial_tile, half_own))
    half_other = lax.ppermute(half_own, "x_lo", swap)
    row_own = call(
        row_normal_kernel, f32(width, span), [SMEM, VMEM, VMEM, VMEM], flops, 2 * 1024 * 1024
    )(place, gathered, half_own, half_other)
    row_other = lax.ppermute(row_own, "core", swap)
    row_normal = call(
        row_sum_kernel,
        jax.ShapeDtypeStruct((width, 3 * span), jnp.bfloat16),
        [VMEM, VMEM],
        scratch=[pltpu.VMEM((SLOTS, width, BLK), jnp.float32)] * 2,
    )(row_own, row_other)
    partial_tile = partial_tile.reshape(cols, width // cols, rows_here)
    arrived = lax.all_to_all(partial_tile, COL, 0, 0, tiled=True)
    row_count = lax.axis_size(ROW)
    inverse_tile, share = call(
        diagonal_kernel,
        (f32(width // cols, rows_here), f32(width // SHARE_PARTS, BLK)),
        [SMEM, VMEM, VMEM],
        flops=2 * 3 * width * span * (width // cols),
        moved=3 * 1024 * 1024,
    )(own_blocks, row_normal, arrived)
    share = share.reshape(row_count, -1, BLK)
    shares = lax.all_to_all(share, ROW, 0, 0, tiled=True)
    diagonal_block = call(
        final_kernel, f32(*pivot_inverse.shape), [VMEM, VMEM], moved=1024 * 128
    )(shares, pivot_inverse)
    return (inverse_tile, diagonal_block)


def solution(mesh):
    finer = Mesh(
        mesh.devices.reshape(2, mesh.shape["row"] // 4, 2, mesh.shape["col"] // 2, 2),
        (*ROW, *COL),
    )
    return jax.shard_map(
        on_device,
        mesh=finer,
        in_specs=(P(ROW, COL), P(COL, ROW), P(ROW, None), P(ROW, COL), P()),
        out_specs=(P(COL, ROW), P(ROW, COL)),
        check_vma=False,
    )
```

```python
import jax
import jax.numpy as jnp
from jax import lax
from jax.experimental import pallas as pl
from jax.experimental.pallas import tpu as pltpu
from jax.sharding import Mesh
from jax.sharding import PartitionSpec as P

BLK = 128
SLOTS = 3
ROW = ("x_hi", "z", "core")
CHIPS = ("x_hi", "z")
COL = ("y", "x_lo")
SMALL = 12 * 1024 * 1024
LARGE = 56 * 1024 * 1024
VMEM = pl.BlockSpec(memory_space=pltpu.VMEM)
SMEM = pl.BlockSpec(memory_space=pltpu.SMEM)
ANY = pl.BlockSpec(memory_space=pl.ANY)
STEPS = 4
SHARE_ROWS = 16
SHARE_PARTS = 4


def split(value):
    high = value.astype(jnp.bfloat16)
    low = (value - high.astype(jnp.float32)).astype(jnp.bfloat16)
    return high, low


def left_parts(value):
    high, low = split(value)
    return jnp.concatenate([high, high, low], axis=1)


def right_parts(value):
    high, low = split(value)
    return jnp.concatenate([high, low, high], axis=0)


def dot(left, right):
    return jnp.dot(left, right, preferred_element_type=jnp.float32)


def spread_kernel(panel, out, held, sems):
    first = pltpu.make_async_copy(panel, held, sems.at[0])
    first.start()
    first.wait()
    copies = [pltpu.make_async_copy(held, out.at[col], sems.at[1 + col]) for col in range(out.shape[0])]
    for copy in copies:
        copy.start()
    for copy in copies:
        copy.wait()


def unit_kernel(place, unit, far, out):
    rows, width = unit.shape
    half = rows // 2
    quarter = width // 4
    start = out.shape[2] - 6 * quarter
    third = jnp.where(place[2] == 0, far[:, 3 * quarter :], unit[:, 2 * quarter : 3 * quarter])
    value = jnp.concatenate([unit[:, : 2 * quarter], third], axis=1)
    for chip in range(out.shape[0]):
        out[chip, :, start : start + 3 * quarter] = value[:half]
        out[chip, :, start + 3 * quarter :] = value[half:]


def pack_kernel(slots, place, stored, before, out):
    del before
    here, half = place[0], place[1]
    chips = out.shape[0]
    rows = stored.shape[1] // 2
    span = SLOTS * BLK

    def block(slot, start):
        index = slots[slot]
        safe = jnp.maximum(index, 0)
        lane = pl.multiple_of(lax.rem(safe, 2) * BLK, BLK)
        value = stored[lax.div(safe, 2), pl.ds(start, rows), pl.ds(lane, BLK)]
        return jnp.where(index >= 0, value, 0.0)

    mine = [block(here * SLOTS + s, part * rows) for part in range(2) for s in range(SLOTS)]
    mine = jnp.concatenate(mine, axis=1)
    start = pl.multiple_of(half * rows, rows)
    for chip in range(chips):
        out[chip, :, : 2 * span] = mine
        for s in range(SLOTS):
            at = 2 * span + s * BLK
            out[chip, :, at : at + BLK] = block(chip * SLOTS + s, start)


def unit_parts(gathered, width):
    quarter = width // 4
    start = gathered.shape[1] - 6 * quarter
    middle = gathered.shape[0] // 2
    zeros = jnp.zeros((middle, 2 * quarter), jnp.float32)
    pieces = []
    for at in (start, start + 3 * quarter):
        pieces.append(jnp.concatenate([gathered[:middle, at : at + 2 * quarter], zeros], axis=1))
        ends = gathered[:middle, at + 2 * quarter : at + 3 * quarter]
        pieces.append(jnp.concatenate([gathered[middle:, at : at + 3 * quarter], ends], axis=1))
    return left_parts(jnp.concatenate(pieces, axis=0).T)


def inverse_kernel(blocks, inverse, out):
    listed = []
    for s in range(SLOTS):
        lane = pl.multiple_of(jnp.maximum(blocks[s], 0) * BLK, BLK)
        listed.append(inverse[:, pl.ds(lane, BLK)].T)
    out[...] = right_parts(jnp.concatenate(listed, axis=0))


def normal_kernel(gathered, out):
    width, span = out.shape
    listed = jnp.concatenate([gathered[:, :span], gathered[:, span : 2 * span]], axis=0)
    out[...] = dot(unit_parts(gathered, width), right_parts(listed))


def row_normal_kernel(place, gathered, own, other, out):
    first = place[1] == 0
    low = jnp.where(first, own[...], other[...])
    high = jnp.where(first, other[...], own[...])
    listed = jnp.concatenate([low, high], axis=0)
    out[...] = dot(unit_parts(gathered, out.shape[0]), right_parts(listed))


def row_sum_kernel(own, other, out, total, ordered):
    width = own.shape[0]
    count = width // SHARE_ROWS
    each = SHARE_ROWS // SHARE_PARTS
    for s in range(SLOTS):
        at = slice(s * BLK, (s + 1) * BLK)
        total[s] = own[:, at] + other[:, at]
        for row in range(SHARE_ROWS):
            part, place = row // each, row % each
            value = total[s, pl.ds(row, count, stride=SHARE_ROWS), :]
            ordered[s, pl.ds(part * count * each + place, count, stride=each), :] = value
    out[...] = left_parts(jnp.concatenate([ordered[s] for s in range(SLOTS)], axis=1))


def window_kernel(inverse, own, other, out, held, made, arrive, leave):
    steps, rows = made.shape[0], made.shape[1]
    at = [slice(t * rows, (t + 1) * rows) for t in range(steps)]
    into = [pltpu.make_async_copy(other.at[at[t]], held.at[t], arrive.at[t]) for t in range(steps)]
    back = [pltpu.make_async_copy(made.at[t], out.at[at[t]], leave.at[t]) for t in range(steps)]
    for copy in into:
        copy.start()
    for t in range(steps):
        into[t].wait()
        made[t] = dot(left_parts(own[at[t]] + held[t]), inverse[...])
        back[t].start()
    for copy in back:
        copy.wait()


def diagonal_kernel(blocks, normal, arrived, tile_out, out):
    tile = arrived[0]
    for c in range(1, arrived.shape[0]):
        tile = tile + arrived[c]
    tile_out[...] = -tile
    listed = []
    for s in range(SLOTS):
        place = blocks[s]
        lane = pl.multiple_of(jnp.maximum(place, 0) * BLK, BLK)
        listed.append(jnp.where(place >= 0, tile_out[:, pl.ds(lane, BLK)], 0.0).T)
    total = dot(normal[...], right_parts(jnp.concatenate(listed, axis=0)))
    rows = out.shape[0]
    out[...] = jnp.concatenate([total[p * rows : (p + 1) * rows] for p in range(SHARE_PARTS)], axis=1)


def final_kernel(arrived, pivot, out):
    total = arrived[0]
    for r in range(1, arrived.shape[0]):
        total = total + arrived[r]
    rows, width = total.shape[0], out.shape[1]
    for p in range(SHARE_PARTS):
        at = slice(p * rows, (p + 1) * rows)
        out[at, :] = pivot[at, :] - total[:, p * width : (p + 1) * width]


def call(kernel, shapes, specs, flops=0, moved=0, aliases=None, outs=VMEM, scratch=(), limit=SMALL):
    return pl.pallas_call(
        kernel,
        out_shape=shapes,
        in_specs=specs,
        out_specs=jax.tree.map(lambda _: outs, shapes),
        scratch_shapes=scratch,
        compiler_params=pltpu.CompilerParams(vmem_limit_bytes=limit),
        input_output_aliases=aliases or {},
        cost_estimate=pl.CostEstimate(flops=flops, bytes_accessed=moved, transcendentals=0),
    )


def f32(*shape):
    return jax.ShapeDtypeStruct(shape, jnp.float32)


def on_device(ancestor_inverse, panel, unit_inverse, pivot_inverse, panel_blocks):
    chip = lax.axis_index(CHIPS)
    core = lax.axis_index("core")
    col = lax.axis_index(COL)
    cols = lax.axis_size(COL)
    chips = lax.axis_size(CHIPS)
    rows_here, cols_here = ancestor_inverse.shape
    unit_rows, width = unit_inverse.shape
    range_blocks = cols_here // BLK
    row_blocks = rows_here // BLK
    span = SLOTS * BLK
    total_blocks = panel_blocks.shape[0]

    owner = panel_blocks // range_blocks
    order = jnp.arange(total_blocks, dtype=jnp.int32)
    same = (owner[:, None] == owner[None, :]) & (order[None, :] < order[:, None])
    slot_of = owner * SLOTS + jnp.sum(same.astype(jnp.int32), axis=1)
    all_slots = jnp.arange(cols * SLOTS, dtype=jnp.int32)
    hit = (slot_of[None, :] == all_slots[:, None]).astype(jnp.int32)
    slots = jnp.sum(hit * (order + 1)[None, :], axis=1) - 1
    window = jnp.sum(hit * (panel_blocks + 1)[None, :], axis=1) - 1
    col_blocks = lax.dynamic_slice(window, (col * SLOTS,), (SLOTS,)) - col * range_blocks
    own_blocks = lax.dynamic_slice(window, (chip * SLOTS,), (SLOTS,))
    own_blocks = own_blocks - chip * range_blocks - core * row_blocks
    own_blocks = jnp.where(own_blocks < row_blocks, own_blocks, -1)
    x_lo = lax.axis_index("x_lo")
    x_hi = lax.axis_index("x_hi")
    place = jnp.stack([col, x_lo, x_hi]).astype(jnp.int32)
    swap = [(0, 1), (1, 0)]
    half = unit_rows // 2
    lanes = 3 * span + 3 * width // 2

    stored = call(
        spread_kernel,
        f32(cols, panel.shape[1], panel.shape[0]),
        [ANY],
        outs=ANY,
        scratch=[
            pltpu.VMEM((panel.shape[1], panel.shape[0]), jnp.float32),
            pltpu.SemaphoreType.DMA((1 + cols,)),
        ],
        limit=LARGE,
    )(panel.T)
    stored = lax.all_to_all(stored, COL, 0, 0, tiled=True)
    far = lax.ppermute(unit_inverse, "x_hi", [(1, 0)])
    before = call(unit_kernel, f32(chips, half, lanes), [SMEM, VMEM, VMEM])(place, unit_inverse, far)
    inverse = call(
        inverse_kernel,
        jax.ShapeDtypeStruct((3 * span, rows_here), jnp.bfloat16),
        [SMEM, VMEM],
        moved=3 * 1024 * 1024,
    )(col_blocks, ancestor_inverse)
    payload = call(
        pack_kernel,
        f32(chips, half, lanes),
        [SMEM, SMEM, VMEM, VMEM],
        moved=1024 * 1024,
        aliases={3: 0},
    )(slots, place, stored, before)
    gathered = lax.all_to_all(payload, CHIPS, 0, 0, tiled=True)
    gathered = gathered.reshape(chips * half, lanes)
    flops = 2 * 3 * chips * unit_rows * width * span
    col_own = call(normal_kernel, f32(width, span), [VMEM], flops, 2 * 1024 * 1024)(gathered)
    col_other = lax.ppermute(col_own, "core", swap)
    step = (STEPS, width // STEPS, rows_here)
    partial_tile = call(
        window_kernel,
        f32(width, rows_here),
        [VMEM, VMEM, ANY],
        flops=2 * 3 * width * span * rows_here,
        moved=3 * 1024 * 1024,
        outs=ANY,
        scratch=[
            pltpu.VMEM((STEPS, width // STEPS, span), jnp.float32),
            pltpu.VMEM(step, jnp.float32),
            pltpu.SemaphoreType.DMA((STEPS,)),
            pltpu.SemaphoreType.DMA((STEPS,)),
        ],
    )(inverse, col_own, col_other)
    half_own = gathered[:, 2 * span : 3 * span]
    partial_tile, half_own = lax.optimization_barrier((partial_tile, half_own))
    half_other = lax.ppermute(half_own, "x_lo", swap)
    row_own = call(
        row_normal_kernel, f32(width, span), [SMEM, VMEM, VMEM, VMEM], flops, 2 * 1024 * 1024
    )(place, gathered, half_own, half_other)
    row_other = lax.ppermute(row_own, "core", swap)
    row_normal = call(
        row_sum_kernel,
        jax.ShapeDtypeStruct((width, 3 * span), jnp.bfloat16),
        [VMEM, VMEM],
        scratch=[pltpu.VMEM((SLOTS, width, BLK), jnp.float32)] * 2,
    )(row_own, row_other)
    partial_tile = partial_tile.reshape(cols, width // cols, rows_here)
    arrived = lax.all_to_all(partial_tile, COL, 0, 0, tiled=True)
    row_count = lax.axis_size(ROW)
    inverse_tile, share = call(
        diagonal_kernel,
        (f32(width // cols, rows_here), f32(width // SHARE_PARTS, BLK)),
        [SMEM, VMEM, VMEM],
        flops=2 * 3 * width * span * (width // cols),
        moved=3 * 1024 * 1024,
    )(own_blocks, row_normal, arrived)
    share = share.reshape(row_count, -1, BLK)
    shares = lax.all_to_all(share, ROW, 0, 0, tiled=True)
    diagonal_block = call(
        final_kernel, f32(*pivot_inverse.shape), [VMEM, VMEM], moved=1024 * 128
    )(shares, pivot_inverse)
    return (inverse_tile, diagonal_block)


def solution(mesh):
    finer = Mesh(
        mesh.devices.reshape(2, mesh.shape["row"] // 4, 2, mesh.shape["col"] // 2, 2),
        (*ROW, *COL),
    )
    return jax.shard_map(
        on_device,
        mesh=finer,
        in_specs=(P(ROW, COL), P(COL, ROW), P(ROW, None), P(ROW, COL), P()),
        out_specs=(P(COL, ROW), P(ROW, COL)),
        check_vma=False,
    )
```

```python
import jax
import jax.numpy as jnp
from jax import lax
from jax.experimental import pallas as pl
from jax.experimental.pallas import tpu as pltpu
from jax.sharding import Mesh
from jax.sharding import PartitionSpec as P

BLK = 128
SLOTS = 3
ROW = ("x_hi", "z", "core")
CHIPS = ("x_hi", "z")
COL = ("y", "x_lo")
SMALL = 12 * 1024 * 1024
LARGE = 56 * 1024 * 1024
VMEM = pl.BlockSpec(memory_space=pltpu.VMEM)
SMEM = pl.BlockSpec(memory_space=pltpu.SMEM)
ANY = pl.BlockSpec(memory_space=pl.ANY)
STEPS = 4
SHARE_ROWS = 16
SHARE_PARTS = 4


def split(value):
    high = value.astype(jnp.bfloat16)
    low = (value - high.astype(jnp.float32)).astype(jnp.bfloat16)
    return high, low


def left_parts(value):
    high, low = split(value)
    return jnp.concatenate([high, high, low], axis=1)


def right_parts(value):
    high, low = split(value)
    return jnp.concatenate([high, low, high], axis=0)


def dot(left, right):
    return jnp.dot(left, right, preferred_element_type=jnp.float32)


def spread_kernel(panel, out, held, sems):
    first = pltpu.make_async_copy(panel, held, sems.at[0])
    first.start()
    first.wait()
    copies = [pltpu.make_async_copy(held, out.at[col], sems.at[1 + col]) for col in range(out.shape[0])]
    for copy in copies:
        copy.start()
    for copy in copies:
        copy.wait()


def unit_kernel(place, unit, far, out):
    rows, width = unit.shape
    half = rows // 2
    quarter = width // 4
    start = out.shape[2] - 6 * quarter
    third = jnp.where(place[2] == 0, far[:, 3 * quarter :], unit[:, 2 * quarter : 3 * quarter])
    value = jnp.concatenate([unit[:, : 2 * quarter], third], axis=1)
    for chip in range(out.shape[0]):
        out[chip, :, start : start + 3 * quarter] = value[:half]
        out[chip, :, start + 3 * quarter :] = value[half:]


def pack_kernel(slots, place, stored, before, out):
    del before
    here, half = place[0], place[1]
    chips = out.shape[0]
    rows = stored.shape[1] // 2
    span = SLOTS * BLK

    def block(slot, start):
        index = slots[slot]
        safe = jnp.maximum(index, 0)
        lane = pl.multiple_of(lax.rem(safe, 2) * BLK, BLK)
        value = stored[lax.div(safe, 2), pl.ds(start, rows), pl.ds(lane, BLK)]
        return jnp.where(index >= 0, value, 0.0)

    mine = [block(here * SLOTS + s, part * rows) for part in range(2) for s in range(SLOTS)]
    mine = jnp.concatenate(mine, axis=1)
    start = pl.multiple_of(half * rows, rows)
    for chip in range(chips):
        out[chip, :, : 2 * span] = mine
        for s in range(SLOTS):
            at = 2 * span + s * BLK
            out[chip, :, at : at + BLK] = block(chip * SLOTS + s, start)


def unit_parts(gathered, width):
    quarter = width // 4
    start = gathered.shape[1] - 6 * quarter
    middle = gathered.shape[0] // 2
    zeros = jnp.zeros((middle, 2 * quarter), jnp.float32)
    pieces = []
    for at in (start, start + 3 * quarter):
        pieces.append(jnp.concatenate([gathered[:middle, at : at + 2 * quarter], zeros], axis=1))
        ends = gathered[:middle, at + 2 * quarter : at + 3 * quarter]
        pieces.append(jnp.concatenate([gathered[middle:, at : at + 3 * quarter], ends], axis=1))
    return left_parts(jnp.concatenate(pieces, axis=0).T)


def inverse_kernel(blocks, inverse, out):
    listed = []
    for s in range(SLOTS):
        lane = pl.multiple_of(jnp.maximum(blocks[s], 0) * BLK, BLK)
        listed.append(inverse[:, pl.ds(lane, BLK)].T)
    out[...] = right_parts(jnp.concatenate(listed, axis=0))


def normal_kernel(gathered, out):
    width, span = out.shape
    listed = jnp.concatenate([gathered[:, :span], gathered[:, span : 2 * span]], axis=0)
    out[...] = dot(unit_parts(gathered, width), right_parts(listed))


def row_normal_kernel(place, gathered, own, other, out):
    first = place[1] == 0
    low = jnp.where(first, own[...], other[...])
    high = jnp.where(first, other[...], own[...])
    listed = jnp.concatenate([low, high], axis=0)
    out[...] = dot(unit_parts(gathered, out.shape[0]), right_parts(listed))


def row_sum_kernel(own, other, out, total, ordered):
    width = own.shape[0]
    count = width // SHARE_ROWS
    each = SHARE_ROWS // SHARE_PARTS
    for s in range(SLOTS):
        at = slice(s * BLK, (s + 1) * BLK)
        total[s] = own[:, at] + other[:, at]
        for row in range(SHARE_ROWS):
            part, place = row // each, row % each
            value = total[s, pl.ds(row, count, stride=SHARE_ROWS), :]
            ordered[s, pl.ds(part * count * each + place, count, stride=each), :] = value
    out[...] = left_parts(jnp.concatenate([ordered[s] for s in range(SLOTS)], axis=1))


def window_kernel(inverse, own, other, out, made, leave):
    steps = made.shape[0]
    rows = made.shape[1]
    copies = []
    for t in range(steps):
        at = slice(t * rows, (t + 1) * rows)
        made[t] = dot(left_parts(own[at] + other[at]), inverse[...])
        copies.append(pltpu.make_async_copy(made.at[t], out.at[at], leave.at[t]))
        copies[t].start()
    for copy in copies:
        copy.wait()


def diagonal_kernel(blocks, normal, arrived, tile_out, out, held, sem):
    tile = arrived[0]
    for c in range(1, arrived.shape[0]):
        tile = tile + arrived[c]
    held[...] = -tile
    copy = pltpu.make_async_copy(held, tile_out, sem.at[0])
    copy.start()
    listed = []
    for s in range(SLOTS):
        place = blocks[s]
        lane = pl.multiple_of(jnp.maximum(place, 0) * BLK, BLK)
        listed.append(jnp.where(place >= 0, held[:, pl.ds(lane, BLK)], 0.0).T)
    total = dot(normal[...], right_parts(jnp.concatenate(listed, axis=0)))
    rows = out.shape[0]
    out[...] = jnp.concatenate([total[p * rows : (p + 1) * rows] for p in range(SHARE_PARTS)], axis=1)
    copy.wait()


def final_kernel(arrived, pivot, out):
    total = arrived[0]
    for r in range(1, arrived.shape[0]):
        total = total + arrived[r]
    rows, width = total.shape[0], out.shape[1]
    for p in range(SHARE_PARTS):
        at = slice(p * rows, (p + 1) * rows)
        out[at, :] = pivot[at, :] - total[:, p * width : (p + 1) * width]


def call(kernel, shapes, specs, flops=0, moved=0, aliases=None, outs=VMEM, scratch=(), limit=SMALL):
    return pl.pallas_call(
        kernel,
        out_shape=shapes,
        in_specs=specs,
        out_specs=outs if isinstance(outs, tuple) else jax.tree.map(lambda _: outs, shapes),
        scratch_shapes=scratch,
        compiler_params=pltpu.CompilerParams(vmem_limit_bytes=limit),
        input_output_aliases=aliases or {},
        cost_estimate=pl.CostEstimate(flops=flops, bytes_accessed=moved, transcendentals=0),
    )


def f32(*shape):
    return jax.ShapeDtypeStruct(shape, jnp.float32)


def on_device(ancestor_inverse, panel, unit_inverse, pivot_inverse, panel_blocks):
    chip = lax.axis_index(CHIPS)
    core = lax.axis_index("core")
    col = lax.axis_index(COL)
    cols = lax.axis_size(COL)
    chips = lax.axis_size(CHIPS)
    rows_here, cols_here = ancestor_inverse.shape
    unit_rows, width = unit_inverse.shape
    range_blocks = cols_here // BLK
    row_blocks = rows_here // BLK
    span = SLOTS * BLK
    total_blocks = panel_blocks.shape[0]

    owner = panel_blocks // range_blocks
    order = jnp.arange(total_blocks, dtype=jnp.int32)
    same = (owner[:, None] == owner[None, :]) & (order[None, :] < order[:, None])
    slot_of = owner * SLOTS + jnp.sum(same.astype(jnp.int32), axis=1)
    all_slots = jnp.arange(cols * SLOTS, dtype=jnp.int32)
    hit = (slot_of[None, :] == all_slots[:, None]).astype(jnp.int32)
    slots = jnp.sum(hit * (order + 1)[None, :], axis=1) - 1
    window = jnp.sum(hit * (panel_blocks + 1)[None, :], axis=1) - 1
    col_blocks = lax.dynamic_slice(window, (col * SLOTS,), (SLOTS,)) - col * range_blocks
    own_blocks = lax.dynamic_slice(window, (chip * SLOTS,), (SLOTS,))
    own_blocks = own_blocks - chip * range_blocks - core * row_blocks
    own_blocks = jnp.where(own_blocks < row_blocks, own_blocks, -1)
    x_lo = lax.axis_index("x_lo")
    x_hi = lax.axis_index("x_hi")
    place = jnp.stack([col, x_lo, x_hi]).astype(jnp.int32)
    swap = [(0, 1), (1, 0)]
    half = unit_rows // 2
    lanes = 3 * span + 3 * width // 2

    stored = call(
        spread_kernel,
        f32(cols, panel.shape[1], panel.shape[0]),
        [ANY],
        outs=ANY,
        scratch=[
            pltpu.VMEM((panel.shape[1], panel.shape[0]), jnp.float32),
            pltpu.SemaphoreType.DMA((1 + cols,)),
        ],
        limit=LARGE,
    )(panel.T)
    stored = lax.all_to_all(stored, COL, 0, 0, tiled=True)
    far = lax.ppermute(unit_inverse, "x_hi", [(1, 0)])
    before = call(unit_kernel, f32(chips, half, lanes), [SMEM, VMEM, VMEM])(place, unit_inverse, far)
    inverse = call(
        inverse_kernel,
        jax.ShapeDtypeStruct((3 * span, rows_here), jnp.bfloat16),
        [SMEM, VMEM],
        moved=3 * 1024 * 1024,
    )(col_blocks, ancestor_inverse)
    stored, inverse = lax.optimization_barrier((stored, inverse))
    payload = call(
        pack_kernel,
        f32(chips, half, lanes),
        [SMEM, SMEM, VMEM, VMEM],
        moved=1024 * 1024,
        aliases={3: 0},
    )(slots, place, stored, before)
    gathered = lax.all_to_all(payload, CHIPS, 0, 0, tiled=True)
    gathered = gathered.reshape(chips * half, lanes)
    flops = 2 * 3 * chips * unit_rows * width * span
    col_own = call(normal_kernel, f32(width, span), [VMEM], flops, 2 * 1024 * 1024)(gathered)
    col_other = lax.ppermute(col_own, "core", swap)
    step = (STEPS, width // STEPS, rows_here)
    partial_tile = call(
        window_kernel,
        f32(width, rows_here),
        [VMEM, VMEM, VMEM],
        flops=2 * 3 * width * span * rows_here,
        moved=3 * 1024 * 1024,
        outs=ANY,
        scratch=[
            pltpu.VMEM(step, jnp.float32),
            pltpu.SemaphoreType.DMA((STEPS,)),
        ],
    )(inverse, col_own, col_other)
    half_own = gathered[:, 2 * span : 3 * span]
    partial_tile, half_own = lax.optimization_barrier((partial_tile, half_own))
    half_other = lax.ppermute(half_own, "x_lo", swap)
    row_own = call(
        row_normal_kernel, f32(width, span), [SMEM, VMEM, VMEM, VMEM], flops, 2 * 1024 * 1024
    )(place, gathered, half_own, half_other)
    row_other = lax.ppermute(row_own, "core", swap)
    row_normal = call(
        row_sum_kernel,
        jax.ShapeDtypeStruct((width, 3 * span), jnp.bfloat16),
        [VMEM, VMEM],
        scratch=[pltpu.VMEM((SLOTS, width, BLK), jnp.float32)] * 2,
    )(row_own, row_other)
    partial_tile = partial_tile.reshape(cols, width // cols, rows_here)
    arrived = lax.all_to_all(partial_tile, COL, 0, 0, tiled=True)
    row_count = lax.axis_size(ROW)
    inverse_tile, share = call(
        diagonal_kernel,
        (f32(width // cols, rows_here), f32(width // SHARE_PARTS, BLK)),
        [SMEM, VMEM, VMEM],
        flops=2 * 3 * width * span * (width // cols),
        moved=3 * 1024 * 1024,
        outs=(ANY, VMEM),
        scratch=[
            pltpu.VMEM((width // cols, rows_here), jnp.float32),
            pltpu.SemaphoreType.DMA((1,)),
        ],
    )(own_blocks, row_normal, arrived)
    share = share.reshape(row_count, -1, BLK)
    shares = lax.all_to_all(share, ROW, 0, 0, tiled=True)
    diagonal_block = call(
        final_kernel, f32(*pivot_inverse.shape), [VMEM, VMEM], moved=1024 * 128
    )(shares, pivot_inverse)
    return (inverse_tile, diagonal_block)


def solution(mesh):
    finer = Mesh(
        mesh.devices.reshape(2, mesh.shape["row"] // 4, 2, mesh.shape["col"] // 2, 2),
        (*ROW, *COL),
    )
    return jax.shard_map(
        on_device,
        mesh=finer,
        in_specs=(P(ROW, COL), P(COL, ROW), P(ROW, None), P(ROW, COL), P()),
        out_specs=(P(COL, ROW), P(ROW, COL)),
        check_vma=False,
    )
```

```python
import jax
import jax.numpy as jnp
from jax import lax
from jax.experimental import pallas as pl
from jax.experimental.pallas import tpu as pltpu
from jax.sharding import Mesh
from jax.sharding import PartitionSpec as P

BLK = 128
SLOTS = 3
ROW = ("x_hi", "z", "core")
CHIPS = ("x_hi", "z")
COL = ("y", "x_lo")
SMALL = 12 * 1024 * 1024
LARGE = 56 * 1024 * 1024
VMEM = pl.BlockSpec(memory_space=pltpu.VMEM)
SMEM = pl.BlockSpec(memory_space=pltpu.SMEM)
ANY = pl.BlockSpec(memory_space=pl.ANY)
STEPS = 8
SHARE_ROWS = 16
SHARE_PARTS = 4


def split(value):
    high = value.astype(jnp.bfloat16)
    low = (value - high.astype(jnp.float32)).astype(jnp.bfloat16)
    return high, low


def left_parts(value):
    high, low = split(value)
    return jnp.concatenate([high, high, low], axis=1)


def right_parts(value):
    high, low = split(value)
    return jnp.concatenate([high, low, high], axis=0)


def dot(left, right):
    return jnp.dot(left, right, preferred_element_type=jnp.float32)


def spread_kernel(panel, out, held, sems):
    first = pltpu.make_async_copy(panel, held, sems.at[0])
    first.start()
    first.wait()
    copies = [pltpu.make_async_copy(held, out.at[col], sems.at[1 + col]) for col in range(out.shape[0])]
    for copy in copies:
        copy.start()
    for copy in copies:
        copy.wait()


def unit_kernel(place, unit, far, out):
    rows, width = unit.shape
    half = rows // 2
    quarter = width // 4
    start = out.shape[2] - 6 * quarter
    third = jnp.where(place[2] == 0, far[:, 3 * quarter :], unit[:, 2 * quarter : 3 * quarter])
    value = jnp.concatenate([unit[:, : 2 * quarter], third], axis=1)
    for chip in range(out.shape[0]):
        out[chip, :, start : start + 3 * quarter] = value[:half]
        out[chip, :, start + 3 * quarter :] = value[half:]


def pack_kernel(slots, place, stored, before, out):
    del before
    here, half = place[0], place[1]
    chips = out.shape[0]
    rows = stored.shape[1] // 2
    span = SLOTS * BLK

    def block(slot, start):
        index = slots[slot]
        safe = jnp.maximum(index, 0)
        lane = pl.multiple_of(lax.rem(safe, 2) * BLK, BLK)
        value = stored[lax.div(safe, 2), pl.ds(start, rows), pl.ds(lane, BLK)]
        return jnp.where(index >= 0, value, 0.0)

    mine = [block(here * SLOTS + s, part * rows) for part in range(2) for s in range(SLOTS)]
    mine = jnp.concatenate(mine, axis=1)
    start = pl.multiple_of(half * rows, rows)
    for chip in range(chips):
        out[chip, :, : 2 * span] = mine
        for s in range(SLOTS):
            at = 2 * span + s * BLK
            out[chip, :, at : at + BLK] = block(chip * SLOTS + s, start)


def unit_parts(gathered, width):
    quarter = width // 4
    start = gathered.shape[1] - 6 * quarter
    middle = gathered.shape[0] // 2
    zeros = jnp.zeros((middle, 2 * quarter), jnp.float32)
    pieces = []
    for at in (start, start + 3 * quarter):
        pieces.append(jnp.concatenate([gathered[:middle, at : at + 2 * quarter], zeros], axis=1))
        ends = gathered[:middle, at + 2 * quarter : at + 3 * quarter]
        pieces.append(jnp.concatenate([gathered[middle:, at : at + 3 * quarter], ends], axis=1))
    return left_parts(jnp.concatenate(pieces, axis=0).T)


def inverse_kernel(blocks, inverse, out):
    listed = []
    for s in range(SLOTS):
        lane = pl.multiple_of(jnp.maximum(blocks[s], 0) * BLK, BLK)
        listed.append(inverse[:, pl.ds(lane, BLK)].T)
    out[...] = right_parts(jnp.concatenate(listed, axis=0))


def normal_kernel(gathered, out):
    width, span = out.shape
    listed = jnp.concatenate([gathered[:, :span], gathered[:, span : 2 * span]], axis=0)
    out[...] = dot(unit_parts(gathered, width), right_parts(listed))


def row_normal_kernel(place, gathered, own, other, out):
    first = place[1] == 0
    low = jnp.where(first, own[...], other[...])
    high = jnp.where(first, other[...], own[...])
    listed = jnp.concatenate([low, high], axis=0)
    out[...] = dot(unit_parts(gathered, out.shape[0]), right_parts(listed))


def row_sum_kernel(own, other, out, total, ordered):
    width = own.shape[0]
    count = width // SHARE_ROWS
    each = SHARE_ROWS // SHARE_PARTS
    for s in range(SLOTS):
        at = slice(s * BLK, (s + 1) * BLK)
        total[s] = own[:, at] + other[:, at]
        for row in range(SHARE_ROWS):
            part, place = row // each, row % each
            value = total[s, pl.ds(row, count, stride=SHARE_ROWS), :]
            ordered[s, pl.ds(part * count * each + place, count, stride=each), :] = value
    out[...] = left_parts(jnp.concatenate([ordered[s] for s in range(SLOTS)], axis=1))


def window_kernel(inverse, own, other, out, made, leave):
    steps = made.shape[0]
    rows = made.shape[1]
    copies = []
    for t in range(steps):
        at = slice(t * rows, (t + 1) * rows)
        made[t] = dot(left_parts(own[at] + other[at]), inverse[...])
        copies.append(pltpu.make_async_copy(made.at[t], out.at[at], leave.at[t]))
        copies[t].start()
    for copy in copies:
        copy.wait()


def diagonal_kernel(blocks, normal, arrived, tile_out, out, held, sem):
    tile = arrived[0]
    for c in range(1, arrived.shape[0]):
        tile = tile + arrived[c]
    held[...] = -tile
    copy = pltpu.make_async_copy(held, tile_out, sem.at[0])
    copy.start()
    listed = []
    for s in range(SLOTS):
        place = blocks[s]
        lane = pl.multiple_of(jnp.maximum(place, 0) * BLK, BLK)
        listed.append(jnp.where(place >= 0, held[:, pl.ds(lane, BLK)], 0.0).T)
    total = dot(normal[...], right_parts(jnp.concatenate(listed, axis=0)))
    rows = out.shape[0]
    out[...] = jnp.concatenate([total[p * rows : (p + 1) * rows] for p in range(SHARE_PARTS)], axis=1)
    copy.wait()


def final_kernel(arrived, pivot, out):
    total = arrived[0]
    for r in range(1, arrived.shape[0]):
        total = total + arrived[r]
    rows, width = total.shape[0], out.shape[1]
    for p in range(SHARE_PARTS):
        at = slice(p * rows, (p + 1) * rows)
        out[at, :] = pivot[at, :] - total[:, p * width : (p + 1) * width]


def call(kernel, shapes, specs, flops=0, moved=0, aliases=None, outs=VMEM, scratch=(), limit=SMALL):
    return pl.pallas_call(
        kernel,
        out_shape=shapes,
        in_specs=specs,
        out_specs=outs if isinstance(outs, tuple) else jax.tree.map(lambda _: outs, shapes),
        scratch_shapes=scratch,
        compiler_params=pltpu.CompilerParams(vmem_limit_bytes=limit),
        input_output_aliases=aliases or {},
        cost_estimate=pl.CostEstimate(flops=flops, bytes_accessed=moved, transcendentals=0),
    )


def f32(*shape):
    return jax.ShapeDtypeStruct(shape, jnp.float32)


def on_device(ancestor_inverse, panel, unit_inverse, pivot_inverse, panel_blocks):
    chip = lax.axis_index(CHIPS)
    core = lax.axis_index("core")
    col = lax.axis_index(COL)
    cols = lax.axis_size(COL)
    chips = lax.axis_size(CHIPS)
    rows_here, cols_here = ancestor_inverse.shape
    unit_rows, width = unit_inverse.shape
    range_blocks = cols_here // BLK
    row_blocks = rows_here // BLK
    span = SLOTS * BLK
    total_blocks = panel_blocks.shape[0]

    owner = panel_blocks // range_blocks
    order = jnp.arange(total_blocks, dtype=jnp.int32)
    same = (owner[:, None] == owner[None, :]) & (order[None, :] < order[:, None])
    slot_of = owner * SLOTS + jnp.sum(same.astype(jnp.int32), axis=1)
    all_slots = jnp.arange(cols * SLOTS, dtype=jnp.int32)
    hit = (slot_of[None, :] == all_slots[:, None]).astype(jnp.int32)
    slots = jnp.sum(hit * (order + 1)[None, :], axis=1) - 1
    window = jnp.sum(hit * (panel_blocks + 1)[None, :], axis=1) - 1
    col_blocks = lax.dynamic_slice(window, (col * SLOTS,), (SLOTS,)) - col * range_blocks
    own_blocks = lax.dynamic_slice(window, (chip * SLOTS,), (SLOTS,))
    own_blocks = own_blocks - chip * range_blocks - core * row_blocks
    own_blocks = jnp.where(own_blocks < row_blocks, own_blocks, -1)
    x_lo = lax.axis_index("x_lo")
    x_hi = lax.axis_index("x_hi")
    place = jnp.stack([col, x_lo, x_hi]).astype(jnp.int32)
    swap = [(0, 1), (1, 0)]
    half = unit_rows // 2
    lanes = 3 * span + 3 * width // 2

    stored = call(
        spread_kernel,
        f32(cols, panel.shape[1], panel.shape[0]),
        [ANY],
        outs=ANY,
        scratch=[
            pltpu.VMEM((panel.shape[1], panel.shape[0]), jnp.float32),
            pltpu.SemaphoreType.DMA((1 + cols,)),
        ],
        limit=LARGE,
    )(panel.T)
    stored = lax.all_to_all(stored, COL, 0, 0, tiled=True)
    far = lax.ppermute(unit_inverse, "x_hi", [(1, 0)])
    before = call(unit_kernel, f32(chips, half, lanes), [SMEM, VMEM, VMEM])(place, unit_inverse, far)
    inverse = call(
        inverse_kernel,
        jax.ShapeDtypeStruct((3 * span, rows_here), jnp.bfloat16),
        [SMEM, VMEM],
        moved=3 * 1024 * 1024,
    )(col_blocks, ancestor_inverse)
    stored, inverse = lax.optimization_barrier((stored, inverse))
    payload = call(
        pack_kernel,
        f32(chips, half, lanes),
        [SMEM, SMEM, VMEM, VMEM],
        moved=1024 * 1024,
        aliases={3: 0},
    )(slots, place, stored, before)
    gathered = lax.all_to_all(payload, CHIPS, 0, 0, tiled=True)
    gathered = gathered.reshape(chips * half, lanes)
    flops = 2 * 3 * chips * unit_rows * width * span
    col_own = call(normal_kernel, f32(width, span), [VMEM], flops, 2 * 1024 * 1024)(gathered)
    col_other = lax.ppermute(col_own, "core", swap)
    step = (STEPS, width // STEPS, rows_here)
    partial_tile = call(
        window_kernel,
        f32(width, rows_here),
        [VMEM, VMEM, VMEM],
        flops=2 * 3 * width * span * rows_here,
        moved=3 * 1024 * 1024,
        outs=ANY,
        scratch=[
            pltpu.VMEM(step, jnp.float32),
            pltpu.SemaphoreType.DMA((STEPS,)),
        ],
    )(inverse, col_own, col_other)
    half_own = gathered[:, 2 * span : 3 * span]
    partial_tile, half_own = lax.optimization_barrier((partial_tile, half_own))
    half_other = lax.ppermute(half_own, "x_lo", swap)
    row_own = call(
        row_normal_kernel, f32(width, span), [SMEM, VMEM, VMEM, VMEM], flops, 2 * 1024 * 1024
    )(place, gathered, half_own, half_other)
    row_other = lax.ppermute(row_own, "core", swap)
    row_normal = call(
        row_sum_kernel,
        jax.ShapeDtypeStruct((width, 3 * span), jnp.bfloat16),
        [VMEM, VMEM],
        scratch=[pltpu.VMEM((SLOTS, width, BLK), jnp.float32)] * 2,
    )(row_own, row_other)
    partial_tile = partial_tile.reshape(cols, width // cols, rows_here)
    arrived = lax.all_to_all(partial_tile, COL, 0, 0, tiled=True)
    row_count = lax.axis_size(ROW)
    inverse_tile, share = call(
        diagonal_kernel,
        (f32(width // cols, rows_here), f32(width // SHARE_PARTS, BLK)),
        [SMEM, VMEM, VMEM],
        flops=2 * 3 * width * span * (width // cols),
        moved=3 * 1024 * 1024,
        outs=(ANY, VMEM),
        scratch=[
            pltpu.VMEM((width // cols, rows_here), jnp.float32),
            pltpu.SemaphoreType.DMA((1,)),
        ],
    )(own_blocks, row_normal, arrived)
    share = share.reshape(row_count, -1, BLK)
    shares = lax.all_to_all(share, ROW, 0, 0, tiled=True)
    diagonal_block = call(
        final_kernel, f32(*pivot_inverse.shape), [VMEM, VMEM], moved=1024 * 128
    )(shares, pivot_inverse)
    return (inverse_tile, diagonal_block)


def solution(mesh):
    finer = Mesh(
        mesh.devices.reshape(2, mesh.shape["row"] // 4, 2, mesh.shape["col"] // 2, 2),
        (*ROW, *COL),
    )
    return jax.shard_map(
        on_device,
        mesh=finer,
        in_specs=(P(ROW, COL), P(COL, ROW), P(ROW, None), P(ROW, COL), P()),
        out_specs=(P(COL, ROW), P(ROW, COL)),
        check_vma=False,
    )
```
